512 devices in a mesh: blk: 16 (over x, z_hi), sub: 32 (over y, z_lo, core).
Axes of the slice: x: 4, y: 8, z: 8 (z_hi: 4, z_lo: 2; z = z_hi * 2 + z_lo), core: 2. Of those that a mesh axis runs over, the one named last changes fastest.
Arguments:
- green: bfloat16 [2, 2, 6, 65536, 512], P(None, None, None, ('blk', 'sub')), may hold values from -6 to 6
- mechanism: float32 [6, 65536], P(None, ('blk', 'sub')), may hold values from -0.009765625 to 0.009765625
- slip: bfloat16 [128, 65536], P(None, ('blk', 'sub')), may hold values from 0.099609375 to 3
- onset: int32 [8, 65536], P(None, ('blk', 'sub')), may hold values from 0 to 1023
- pattern_of_variation: int32 [512], replicated, may hold values from 0 to 127
- hypo_of_variation: int32 [512], replicated, may hold values from 0 to 7
Outputs:
- seismograms: float32 [512, 2, 1024], P(('blk', 'sub'))
The draws below stay inside these ranges and needn't reach their ends.
All inputs are finite; a program needn't handle non-finite values.
Results may differ from the reference program's by a relative error of at most 0.0029.
Values may be sent and summed in bfloat16 or wider, within the bound.
No kernel may reach another device: no remote copies, remote signals or barrier semaphores. Data moves between devices by JAX's collectives and lax.ppermute only.
A program may use at most 64 MiB of HBM per device.

```python
import math
import jax
import jax.numpy as jnp
from jax import lax

NT = 1024
F = 512
C = 2
K = 6
P_SIZE = 128
H = 8
SUBFAULTS = 65536
R = 512


def touch_ends(values, key, least, top_value):
    place = [jax.random.randint(jax.random.fold_in(key, axis), (), 0, length) for axis, length in enumerate(values.shape)]
    longest = values.shape.index(max(values.shape))
    neighbour = place[:longest] + [(place[longest] + 1) % values.shape[longest]] + place[longest + 1:]
    return values.at[tuple(place)].set(least).at[tuple(neighbour)].set(top_value)


def level_of(rng, extent, pieces, low, largest):
    gain, own = 1.0, jax.random.fold_in(rng, 6)
    for dim, shards_of in pieces:
        heights = jnp.exp(jax.random.uniform(jax.random.fold_in(own, dim), (shards_of,), jnp.float32, low / len(pieces), largest / len(pieces)))
        gain = gain * jnp.repeat(heights, extent[dim] // shards_of).reshape([-1 if axis == dim else 1 for axis in range(len(extent))])
    return gain


def scatter_about(key, shape, width, most, pieces=(), kind=jnp.bfloat16):
    loudness = level_of(key, shape, pieces, -0.22, 0.18) if pieces else 1.0
    entries = jax.random.normal(key, shape, jnp.float32) * width * loudness
    return jnp.minimum(jnp.maximum(entries, -most), most).astype(kind)


def setup_inputs(seed: int = 0) -> dict:
    arg_keys = jax.random.split(jax.random.key(seed), 7)
    green = scatter_about(arg_keys[0], (2, C, K, SUBFAULTS, F), 1.0, 6.0, ((3, 512),))
    mechanism = scatter_about(arg_keys[1], (K, SUBFAULTS), (K * SUBFAULTS) ** -0.5, 0.009765625, ((1, 512),), jnp.float32)
    slip = jnp.clip(jnp.exp(math.log(3.0) - 3.4051113 * jax.random.uniform(arg_keys[2], (P_SIZE, SUBFAULTS), jnp.float32) ** level_of(arg_keys[2], (P_SIZE, SUBFAULTS), ((1, 512),), -0.2, 0.2)), 0.099609375, 3.0).astype(jnp.bfloat16)
    onset = touch_ends(jax.random.randint(arg_keys[3], (H, SUBFAULTS), 0, NT), jax.random.fold_in(arg_keys[3], 1), 0, NT - 1).astype(jnp.int32)
    pattern_of_variation = touch_ends(jax.random.randint(arg_keys[4], (R,), 0, P_SIZE), jax.random.fold_in(arg_keys[4], 1), 0, P_SIZE - 1).astype(jnp.int32)
    hypo_of_variation = touch_ends(jax.random.randint(arg_keys[5], (R,), 0, H), jax.random.fold_in(arg_keys[5], 1), 0, H - 1).astype(jnp.int32)
    return {"green": green, "mechanism": mechanism, "slip": slip, "onset": onset, "pattern_of_variation": pattern_of_variation, "hypo_of_variation": hypo_of_variation}


def inverse_table(freq_count, samples):
    freq = jnp.arange(freq_count, dtype=jnp.int32)
    times = jnp.arange(samples, dtype=jnp.int32)
    steps = freq[:, None] * times[None, :] % samples
    angle = steps.astype(jnp.float32) * (2.0 * math.pi / samples)
    weight = jnp.where(freq == 0, 0.5, 1.0).astype(jnp.float32) / math.sqrt(freq_count)
    return jnp.concatenate([weight[:, None] * jnp.cos(angle), -weight[:, None] * jnp.sin(angle)], axis=0)

def reference(green, mechanism, slip, onset, pattern_of_variation, hypo_of_variation):
    freq_count = green.shape[4]
    samples = 2 * freq_count
    merged = lax.optimization_barrier(jnp.sum(mechanism[None, None, :, :, None] * green.astype(jnp.float32), axis=2))
    real_part = jnp.transpose(merged[0], (1, 0, 2))
    imag_part = jnp.transpose(merged[1], (1, 0, 2))
    freq = jnp.arange(freq_count, dtype=jnp.int32)

    def per_hypo(onset_row):
        steps = onset_row[:, None] * freq[None, :] % samples
        angle = steps.astype(jnp.float32) * (2.0 * math.pi / samples)
        cosine = jnp.cos(angle)[:, None, :]
        sine = jnp.sin(angle)[:, None, :]
        shifted_re = cosine * real_part + sine * imag_part
        shifted_im = cosine * imag_part - sine * real_part
        shifted = jnp.stack([shifted_re, shifted_im], axis=2).astype(jnp.bfloat16)
        shifted = shifted.reshape(shifted.shape[0], -1)
        return jnp.dot(slip, shifted, preferred_element_type=jnp.float32)
    table = lax.map(per_hypo, onset)
    table = table.reshape(-1, table.shape[2])
    combos = (hypo_of_variation * slip.shape[0] + pattern_of_variation).astype(jnp.int32)
    spectra = jnp.take(table, combos, axis=0)
    count = spectra.shape[0]
    rows = spectra.reshape(count * green.shape[1], 2 * freq_count)
    result = jnp.dot(rows, inverse_table(freq_count, samples), precision=lax.Precision.HIGHEST, preferred_element_type=jnp.float32)
    return result.reshape(count, green.shape[1], samples)
```

```python
import math

import jax
import jax.numpy as jnp
import numpy as np
from jax import lax
from jax.experimental import pallas as pl
from jax.experimental.pallas import tpu as pltpu
from jax.sharding import Mesh
from jax.sharding import PartitionSpec as P

AXES = ("x", "zh", "y", "zl", "c")
GROUP = ("x", "c")
PLANE = ("zh", "y", "zl")
CODE_TOP = 32000.0
SLIP_UNIT = 2048.0
LEAST = 4e-34
F32, BF16, I32, I16 = jnp.float32, jnp.bfloat16, jnp.int32, jnp.int16
VMEM = 48 * 1024 * 1024


def cos_sin(steps, samples):
    eighth = samples // 8
    quadrant = (steps + eighth) >> int(math.log2(samples // 4))
    rest = steps - quadrant * (samples // 4)
    t = rest.astype(F32) * (2.0 * math.pi / samples)
    t2 = t * t
    sine = t + t * t2 * (-1.0 / 6 + t2 * (1.0 / 120 + t2 * (-1.0 / 5040 + t2 * (1.0 / 362880))))
    cosine = 1.0 + t2 * (-0.5 + t2 * (1.0 / 24 + t2 * (-1.0 / 720 + t2 * (1.0 / 40320))))
    odd = (quadrant & 1) == 1
    c = jnp.where(odd, sine, cosine)
    s = jnp.where(odd, cosine, sine)
    c = jnp.where(((quadrant + 1) & 2) == 2, -c, c)
    s = jnp.where((quadrant & 2) == 2, -s, s)
    return c, s


def merge_kernel(groups, green_ref, mech_ref, slip_ref, onset_ref, msg_ref, cols, merged, top):
    step = pl.program_id(0) * pl.num_programs(1) + pl.program_id(1)
    kinds, subs, freqs = green_ref.shape[2:]
    share = freqs // groups

    @pl.when(step == 0)
    def _():
        for k in range(kinds):
            cols[k] = jnp.broadcast_to(mech_ref[k : k + 1, :], (subs, subs)).T
        top[...] = jnp.zeros_like(top)

    for tile in range(freqs // subs):
        lanes = pl.ds(tile * subs, subs)
        total = cols[0] * green_ref[0, 0, 0, :, lanes].astype(F32)
        for k in range(1, kinds):
            total = total + cols[k] * green_ref[0, 0, k, :, lanes].astype(F32)
        total = total.T
        merged[step, lanes, :] = total
        top[...] = jnp.maximum(top[...], jnp.max(jnp.abs(total).reshape(subs // 8, 8, subs), axis=0))

    @pl.when(step == 3)
    def _():
        most = jnp.maximum(jnp.max(top[...], axis=0, keepdims=True), LEAST)
        power = jnp.ceil(jnp.log2(most * (1.0 / CODE_TOP)))
        power = jnp.maximum(power, -126.0)
        inverse = jnp.exp2(-power)
        slip = (slip_ref[...].astype(F32) * SLIP_UNIT).astype(I32).astype(I16)
        head = jnp.concatenate([onset_ref[...], jnp.broadcast_to(power.astype(I32), (8, subs))], axis=0).astype(I16)
        for g in range(groups):
            for i in range(4):
                part = merged[i, pl.ds(g, share, stride=groups), :] * inverse
                msg_ref[g, i * share : (i + 1) * share, :] = jnp.round(part).astype(I32).astype(I16)
            msg_ref[g, 4 * share : 4 * share + 128, :] = slip
            msg_ref[g, 4 * share + 128 : 4 * share + 144, :] = head


def table_kernel(groups, samples, place_ref, msg_ref, combo_ref, out_ref, slips, shifted, table):
    share = samples // 2 // groups
    hypos = shifted.shape[0]
    subs = msg_ref.shape[2]
    mine = place_ref[0]
    freq = mine + groups * lax.broadcasted_iota(I32, (16, subs), 0)

    def one_source(src, carry):
        lanes = pl.ds(pl.multiple_of(src * subs, subs), subs)
        slip = msg_ref[src, 4 * share : 4 * share + 128, :].astype(I32).astype(F32) * (1.0 / SLIP_UNIT)
        slips[:, lanes] = slip.astype(BF16)
        head = msg_ref[src, 4 * share + 128 : 4 * share + 144, :].astype(I32)
        unit = jnp.exp2(head[8:9].astype(F32))
        jump_c, jump_s = cos_sin((head[0:8] * (16 * groups)) & (samples - 1), samples)
        for h in range(hypos):
            onset = jnp.broadcast_to(head[h : h + 1], (16, subs))
            cosine, sine = cos_sin((onset * freq) & (samples - 1), samples)
            cosine, sine = cosine * unit, sine * unit
            jc = jnp.broadcast_to(jump_c[h : h + 1], (16, subs))
            js = jnp.broadcast_to(jump_s[h : h + 1], (16, subs))
            for a in range(share // 16):
                if a:
                    cosine, sine = cosine * jc - sine * js, sine * jc + cosine * js
                for comp in range(2):
                    r0 = comp * share + a * 16
                    re = msg_ref[src, r0 : r0 + 16, :].astype(I32).astype(F32)
                    im = msg_ref[src, 2 * share + r0 : 2 * share + r0 + 16, :].astype(I32).astype(F32)
                    x0 = comp * 2 * share + a * 16
                    shifted[h, x0 : x0 + 16, lanes] = (cosine * re + sine * im).astype(BF16)
                    shifted[h, x0 + share : x0 + share + 16, lanes] = (cosine * im - sine * re).astype(BF16)
        return carry

    lax.fori_loop(0, groups, one_source, 0)
    pats = slips.shape[0]
    for h in range(hypos):
        rows = lax.dot_general(slips[...], shifted[h], (((1,), (1,)), ((), ())), preferred_element_type=F32)
        table[h * pats : (h + 1) * pats, :] = rows.astype(BF16)
    combo = combo_ref[...]
    chosen = jnp.zeros(out_ref.shape[:1] + (1,), F32)
    count = combo.shape[0]
    spectra = None
    for h in range(hypos):
        ids = lax.broadcasted_iota(I32, (count, pats), 1) + h * pats
        pick = jnp.where(combo == ids, 1.0, 0.0).astype(BF16)
        term = jnp.dot(pick, table[h * pats : (h + 1) * pats, :], preferred_element_type=F32)
        spectra = term if spectra is None else spectra + term
    dests = out_ref.shape[0]
    parts = [spectra[:, i * 128 : (i + 1) * 128].reshape(dests, count // dests, 128) for i in range(spectra.shape[1] // 128)]
    out_ref[...] = jnp.concatenate(parts, axis=1).astype(BF16)


def sum_kernel(in_ref, out_ref):
    total = jnp.sum(in_ref[...].astype(F32), axis=0)
    rows = out_ref.shape[0]
    for i in range(rows):
        for half in range(2):
            out_ref[i, half : half + 1, :] = total[half * rows + i : half * rows + i + 1, :]


def inverse_tables(groups, freqs, samples):
    share = freqs // groups
    k, b, g, a = np.arange(share), np.arange(128), np.arange(groups), np.arange(samples // 128)
    turn = 2.0 * math.pi / samples
    first = turn * (groups * k[:, None] * b[None, :] % samples)
    c, s = np.cos(first), np.sin(first)
    main = np.concatenate([np.concatenate([c, s], 1), np.concatenate([-s, c], 1)], 0) / math.sqrt(freqs)
    second = np.repeat(turn * (g[:, None] * b[None, :] % samples), 2, axis=0)
    twist = np.stack([np.cos(second), np.sin(second)])
    third = turn * (128 * g[:, None] * a[None, :] % samples)
    last = np.stack([np.cos(third), -np.sin(third)])[..., None] * np.ones((1, 1, 1, 128))
    return [t.astype(np.float32) for t in (main, twist, last)]


def inverse_kernel(in_ref, main_ref, twist_ref, last_ref, out_ref):
    groups, comps, width = in_ref.shape
    rows = in_ref[...].reshape(groups * comps, width)
    row = lax.broadcasted_iota(I32, rows.shape, 0)
    lane = lax.broadcasted_iota(I32, rows.shape, 1)
    rows = jnp.where((row < comps) & (lane % (width // 2) == 0), 0.5 * rows, rows)
    v = jnp.dot(rows, main_ref[...], precision=lax.Precision.HIGHEST, preferred_element_type=F32)
    vr, vi = v[:, :128], v[:, 128:]
    c, s = twist_ref[0], twist_ref[1]
    ur, ui = vr * c - vi * s, vr * s + vi * c
    for comp in range(comps):
        total = None
        for g in range(groups):
            r = g * comps + comp
            term = last_ref[0, g] * ur[r : r + 1] + last_ref[1, g] * ui[r : r + 1]
            total = term if total is None else total + term
        for a in range(total.shape[0]):
            out_ref[0, comp : comp + 1, a * 128 : (a + 1) * 128] = total[a : a + 1]


def on_device(green, mechanism, slip, onset, pattern_of_variation, hypo_of_variation):
    _, comps, kinds, subs, freqs = green.shape
    samples = 2 * freqs
    pats, hypos = slip.shape[0], onset.shape[0]
    groups = lax.axis_size(GROUP)
    planes = lax.axis_size(PLANE)
    count = pattern_of_variation.shape[0]
    share = freqs // groups
    lines = 4 * share + pats + 16
    params = pltpu.CompilerParams(vmem_limit_bytes=VMEM)

    msg = pl.pallas_call(
        lambda *refs: merge_kernel(groups, *refs),
        out_shape=jax.ShapeDtypeStruct((groups, lines, subs), I16),
        grid=(2, comps),
        in_specs=[
            pl.BlockSpec((1, 1, kinds, subs, freqs), lambda q, c: (q, c, 0, 0, 0)),
            pl.BlockSpec((kinds, subs), lambda q, c: (0, 0)),
            pl.BlockSpec((pats, subs), lambda q, c: (0, 0)),
            pl.BlockSpec((hypos, subs), lambda q, c: (0, 0)),
        ],
        out_specs=pl.BlockSpec((groups, lines, subs), lambda q, c: (0, 0, 0)),
        scratch_shapes=[
            pltpu.VMEM((kinds, subs, subs), F32),
            pltpu.VMEM((2 * comps, freqs, subs), F32),
            pltpu.VMEM((8, subs), F32),
        ],
        compiler_params=params,
        name="merge",
    )(green, mechanism, slip, onset)

    msg = lax.all_to_all(msg, GROUP, 0, 0, tiled=True)

    combos = hypo_of_variation * pats + pattern_of_variation
    gx, gc = lax.axis_size("x"), lax.axis_size("c")
    combos = combos.reshape(gx, planes, gc).transpose(1, 0, 2).reshape(count, 1)
    place = lax.axis_index(GROUP).astype(I32).reshape(1)
    width = 4 * share
    parts = pl.pallas_call(
        lambda *refs: table_kernel(groups, samples, *refs),
        out_shape=jax.ShapeDtypeStruct((planes, count // planes * (width // 128), 128), BF16),
        in_specs=[
            pl.BlockSpec(memory_space=pltpu.SMEM),
            pl.BlockSpec(memory_space=pltpu.VMEM),
            pl.BlockSpec(memory_space=pltpu.VMEM),
        ],
        out_specs=pl.BlockSpec(memory_space=pltpu.VMEM),
        scratch_shapes=[
            pltpu.VMEM((pats, groups * subs), BF16),
            pltpu.VMEM((hypos, width, groups * subs), BF16),
            pltpu.VMEM((hypos * pats, width), BF16),
        ],
        compiler_params=params,
        name="table",
    )(place, msg, combos)

    parts = lax.all_to_all(parts, PLANE, 0, 0, tiled=True)

    summed = pl.pallas_call(
        sum_kernel,
        out_shape=jax.ShapeDtypeStruct((count // planes, width // 128, 128), F32),
        compiler_params=params,
        name="sum",
    )(parts)

    spectra = lax.all_to_all(summed, GROUP, 0, 0, tiled=True)

    tables = [jnp.asarray(t) for t in inverse_tables(groups, freqs, samples)]
    return pl.pallas_call(
        inverse_kernel,
        out_shape=jax.ShapeDtypeStruct((1, comps, samples), F32),
        compiler_params=params,
        name="inverse",
    )(spectra, *tables)


def solution(mesh):
    blk, sub = mesh.devices.shape
    fine = Mesh(mesh.devices.reshape(4, blk // 4, sub // 4, 2, 2), AXES)
    in_specs = (
        P(None, None, None, AXES, None),
        P(None, AXES),
        P(None, AXES),
        P(None, AXES),
        P(),
        P(),
    )
    out_specs = P(AXES, None, None)
    return jax.shard_map(on_device, mesh=fine, in_specs=in_specs, out_specs=out_specs, check_vma=False)
```

```python
import math

import jax
import jax.numpy as jnp
import numpy as np
from jax import lax
from jax.experimental import pallas as pl
from jax.experimental.pallas import tpu as pltpu
from jax.sharding import Mesh
from jax.sharding import PartitionSpec as P

AXES = ("x", "zh", "y", "zl", "c")
GROUP = ("x", "c")
PLANE = ("zh", "y", "zl")
CODE_TOP = 32000.0
SLIP_UNIT = 2048.0
LEAST = 4e-34
F32, BF16, I32, I16 = jnp.float32, jnp.bfloat16, jnp.int32, jnp.int16
VMEM = 48 * 1024 * 1024
MERGE_VMEM = 63 * 1024 * 1024


def cos_sin(steps, samples):
    eighth = samples // 8
    quadrant = (steps + eighth) >> int(math.log2(samples // 4))
    rest = steps - quadrant * (samples // 4)
    t = rest.astype(F32) * (2.0 * math.pi / samples)
    t2 = t * t
    sine = t + t * t2 * (-1.0 / 6 + t2 * (1.0 / 120 + t2 * (-1.0 / 5040 + t2 * (1.0 / 362880))))
    cosine = 1.0 + t2 * (-0.5 + t2 * (1.0 / 24 + t2 * (-1.0 / 720 + t2 * (1.0 / 40320))))
    odd = (quadrant & 1) == 1
    c = jnp.where(odd, sine, cosine)
    s = jnp.where(odd, cosine, sine)
    c = jnp.where(((quadrant + 1) & 2) == 2, -c, c)
    s = jnp.where((quadrant & 2) == 2, -s, s)
    return c, s


def merge_kernel(groups, green_ref, mech_ref, slip_ref, onset_ref, out_ref, green, mech, slip, onset, merged, msg, sems, out_sems):
    _, comps, kinds, subs, freqs = green_ref.shape
    share = freqs // groups
    end = 2 * comps * share
    blocks = [(c, q) for c in range(comps) for q in range(2)]
    copies = [pltpu.make_async_copy(mech_ref, mech, sems.at[0])]
    for i, (c, q) in enumerate(blocks):
        copies.append(pltpu.make_async_copy(green_ref.at[q, c], green.at[i], sems.at[1 + i]))
    copies.append(pltpu.make_async_copy(slip_ref, slip, sems.at[1 + 2 * comps]))
    copies.append(pltpu.make_async_copy(onset_ref, onset, sems.at[2 + 2 * comps]))
    for copy in copies:
        copy.start()
    copies[0].wait()
    cols = [jnp.broadcast_to(mech[k : k + 1, :], (subs, subs)).T for k in range(kinds)]
    powers, sends = [], []
    for i in range(2 * comps):
        copies[1 + i].wait()
        top = jnp.zeros((8, subs), F32)
        for tile in range(freqs // subs):
            piece = slice(tile * subs, (tile + 1) * subs)
            total = cols[0] * green[i, 0, :, piece].astype(F32)
            for k in range(1, kinds):
                total = total + cols[k] * green[i, k, :, piece].astype(F32)
            total = total.T
            merged[i, piece, :] = total
            top = jnp.maximum(top, jnp.max(jnp.abs(total).reshape(subs // 8, 8, subs), axis=0))
        most = jnp.maximum(jnp.max(top, axis=0, keepdims=True), LEAST)
        power = jnp.maximum(jnp.ceil(jnp.log2(most * (1.0 / CODE_TOP))), -126.0)
        powers.append(power.astype(I32))
        inverse = jnp.exp2(-power)
        lines = slice(i * share, (i + 1) * share)
        for g in range(groups):
            part = merged[i, pl.ds(g, share, stride=groups), :] * inverse
            msg[g, lines, :] = jnp.round(part).astype(I32).astype(I16)
        sends.append(pltpu.make_async_copy(msg.at[:, lines], out_ref.at[:, lines], out_sems.at[i]))
        sends[-1].start()
        if i == 0:
            copies[-2].wait()
            codes = (slip[...].astype(F32) * SLIP_UNIT).astype(I32).astype(I16)
            for g in range(groups):
                msg[g, end + 16 :, :] = codes
            tail = slice(end + 16, msg.shape[1])
            sends.append(pltpu.make_async_copy(msg.at[:, tail], out_ref.at[:, tail], out_sems.at[2 * comps]))
            sends[-1].start()
    copies[-1].wait()
    head = jnp.concatenate([jnp.broadcast_to(p, (8 // len(powers), subs)) for p in powers] + [onset[...]], axis=0).astype(I16)
    for g in range(groups):
        msg[g, end : end + 16, :] = head
    sends.append(pltpu.make_async_copy(msg.at[:, end : end + 16], out_ref.at[:, end : end + 16], out_sems.at[2 * comps + 1]))
    sends[-1].start()
    for send in sends:
        send.wait()


def pick_kernel(combo_ref, pick_ref):
    count, entries = pick_ref.shape
    for first in range(0, entries, 128):
        ids = lax.broadcasted_iota(I32, (count, 128), 1) + first
        pick_ref[:, first : first + 128] = jnp.where(combo_ref[...] == ids, 1.0, 0.0).astype(BF16)


def table_kernel(groups, samples, place_ref, msg_ref, pick_ref, out_ref, slips, values, shifted, turns):
    hypos, rows, _ = shifted.shape
    subs = values.shape[2]
    pats = slips.shape[0]
    share = rows // 4
    mine = place_ref[0]
    freq = mine + groups * lax.broadcasted_iota(I32, (8, subs), 0)

    for src in range(groups):
        lanes = slice(src * subs, (src + 1) * subs)
        slip = msg_ref[src, rows + 16 :, :].astype(I32).astype(F32) * (1.0 / SLIP_UNIT)
        slips[:, lanes] = slip.astype(BF16)
        head = msg_ref[src, rows : rows + 16, :].astype(I32)
        for i in range(4):
            lines = slice(i * share, (i + 1) * share)
            unit = jnp.exp2(head[2 * i : 2 * i + 1].astype(F32))
            values[src, lines, :] = msg_ref[src, lines, :].astype(I32).astype(F32) * unit
        near_c, near_s = cos_sin((head[8:16] * (8 * groups)) & (samples - 1), samples)
        turns[src, 0] = near_c
        turns[src, 1] = near_s
        turns[src, 2] = near_c * near_c - near_s * near_s
        turns[src, 3] = 2.0 * near_c * near_s

    spectra = None
    for h in range(hypos):
        for src in range(groups):
            lanes = slice(src * subs, (src + 1) * subs)
            row = rows + 8 + h
            onset = jnp.broadcast_to(msg_ref[src, rows : rows + 16, :].astype(I32)[8 + h : 9 + h], (8, subs))
            c0, s0 = cos_sin((onset * freq) & (samples - 1), samples)
            nc, ns = turns[src, 0, h : h + 1, :], turns[src, 1, h : h + 1, :]
            c = jnp.concatenate([c0, c0 * nc - s0 * ns], axis=0)
            s = jnp.concatenate([s0, s0 * nc + c0 * ns], axis=0)
            jc = jnp.broadcast_to(turns[src, 2, h : h + 1, :], (16, subs))
            js = jnp.broadcast_to(turns[src, 3, h : h + 1, :], (16, subs))
            for a in range(share // 16):
                if a:
                    c, s = c * jc - s * js, s * jc + c * js
                for comp in range(2):
                    r0 = comp * 2 * share + a * 16
                    re = values[src, r0 : r0 + 16, :]
                    im = values[src, r0 + share : r0 + share + 16, :]
                    shifted[h, r0 : r0 + 16, lanes] = (c * re + s * im).astype(BF16)
                    shifted[h, r0 + share : r0 + share + 16, lanes] = (c * im - s * re).astype(BF16)
        sums = lax.dot_general(slips[...], shifted[h], (((1,), (1,)), ((), ())), preferred_element_type=F32)
        sums = sums.astype(BF16)
        if h % 2 == 0:
            held = sums
        else:
            both = jnp.concatenate([held, sums], axis=0)
            chosen = jnp.dot(pick_ref[:, (h - 1) * pats : (h + 1) * pats], both, preferred_element_type=F32)
            spectra = chosen if spectra is None else spectra + chosen
    dests = out_ref.shape[0]
    parts = [spectra[:, i : i + 128].reshape(dests, -1, 128) for i in range(0, rows, 128)]
    out_ref[...] = jnp.concatenate(parts, axis=1).astype(BF16)


def sum_kernel(in_ref, out_ref):
    total = jnp.sum(in_ref[...].astype(F32), axis=0)
    rows = out_ref.shape[0]
    for i in range(rows):
        for half in range(2):
            out_ref[i, half : half + 1, :] = total[half * rows + i : half * rows + i + 1, :]


def inverse_tables(groups, freqs, samples):
    share = freqs // groups
    k, b, g, a = np.arange(share), np.arange(128), np.arange(groups), np.arange(samples // 128)
    turn = 2.0 * math.pi / samples
    first = turn * (groups * k[:, None] * b[None, :] % samples)
    c, s = np.cos(first), np.sin(first)
    main = np.concatenate([np.concatenate([c, s], 1), np.concatenate([-s, c], 1)]) / math.sqrt(freqs)
    second = np.tile(turn * (g[:, None] * b[None, :] % samples), (2, 1))
    twist = np.stack([np.cos(second), np.sin(second)])
    third = turn * (128 * g[:, None] * a[None, :] % samples)
    last = np.stack([np.cos(third), -np.sin(third)])[..., None] * np.ones((1, 1, 1, 128))
    return [t.astype(np.float32) for t in (main, twist, last)]


def inverse_kernel(in_ref, main_ref, twist_ref, last_ref, out_ref):
    groups, comps, width = in_ref.shape
    rows = jnp.concatenate([in_ref[:, comp, :] for comp in range(comps)], axis=0)
    row = lax.broadcasted_iota(I32, rows.shape, 0)
    lane = lax.broadcasted_iota(I32, rows.shape, 1)
    zero = (row % groups == 0) & (lane % (width // 2) == 0)
    rows = jnp.where(zero, 0.5 * rows, rows)
    v = jnp.dot(rows, main_ref[...], precision=lax.Precision.HIGHEST, preferred_element_type=F32)
    vr, vi = v[:, :128], v[:, 128:]
    c, s = twist_ref[0], twist_ref[1]
    ur, ui = vr * c - vi * s, vr * s + vi * c
    for comp in range(comps):
        total = None
        for g in range(groups):
            r = comp * groups + g
            term = last_ref[0, g] * ur[r : r + 1] + last_ref[1, g] * ui[r : r + 1]
            total = term if total is None else total + term
        for a in range(total.shape[0]):
            out_ref[0, comp : comp + 1, a * 128 : (a + 1) * 128] = total[a : a + 1]


def merge_call(groups, green, mechanism, slip, onset):
    _, comps, kinds, subs, freqs = green.shape
    pats, hypos = slip.shape[0], onset.shape[0]
    lines = 2 * comps * freqs // groups + 16 + pats
    return pl.pallas_call(
        lambda *refs: merge_kernel(groups, *refs),
        out_shape=jax.ShapeDtypeStruct((groups, lines, subs), I16),
        in_specs=[pl.BlockSpec(memory_space=pltpu.HBM)] * 4,
        out_specs=pl.BlockSpec(memory_space=pltpu.HBM),
        scratch_shapes=[
            pltpu.VMEM((2 * comps, kinds, subs, freqs), BF16),
            pltpu.VMEM((kinds, subs), F32),
            pltpu.VMEM((pats, subs), BF16),
            pltpu.VMEM((hypos, subs), I32),
            pltpu.VMEM((2 * comps, freqs, subs), F32),
            pltpu.VMEM((groups, lines, subs), I16),
            pltpu.SemaphoreType.DMA((2 * comps + 3,)),
            pltpu.SemaphoreType.DMA((2 * comps + 2,)),
        ],
        compiler_params=pltpu.CompilerParams(vmem_limit_bytes=MERGE_VMEM),
        name="merge",
    )(green, mechanism, slip, onset)


def table_call(groups, samples, planes, hypos, pats, place, msg, pick):
    subs = msg.shape[2]
    rows = msg.shape[1] - 16 - pats
    in_vmem = pl.BlockSpec(memory_space=pltpu.VMEM)
    return pl.pallas_call(
        lambda *refs: table_kernel(groups, samples, *refs),
        out_shape=jax.ShapeDtypeStruct((planes, pick.shape[0] // planes * (rows // 128), 128), BF16),
        in_specs=[pl.BlockSpec(memory_space=pltpu.SMEM), in_vmem, in_vmem],
        out_specs=in_vmem,
        scratch_shapes=[
            pltpu.VMEM((pats, groups * subs), BF16),
            pltpu.VMEM((groups, rows, subs), F32),
            pltpu.VMEM((hypos, rows, groups * subs), BF16),
            pltpu.VMEM((groups, 4, hypos, subs), F32),
        ],
        compiler_params=pltpu.CompilerParams(vmem_limit_bytes=VMEM),
        name="table",
    )(place, msg, pick)


def on_device(green, mechanism, slip, onset, pattern_of_variation, hypo_of_variation):
    _, comps, kinds, subs, freqs = green.shape
    samples = 2 * freqs
    pats, hypos = slip.shape[0], onset.shape[0]
    groups = lax.axis_size(GROUP)
    planes = lax.axis_size(PLANE)
    count = pattern_of_variation.shape[0]
    rows = 2 * comps * freqs // groups
    params = pltpu.CompilerParams(vmem_limit_bytes=VMEM)
    in_vmem = pl.BlockSpec(memory_space=pltpu.VMEM)

    msg = merge_call(groups, green, mechanism, slip, onset)
    msg = lax.all_to_all(msg, GROUP, 0, 0, tiled=True)

    combos = hypo_of_variation * pats + pattern_of_variation
    gx, gc = lax.axis_size("x"), lax.axis_size("c")
    combos = combos.reshape(gx, planes, gc).transpose(1, 0, 2).reshape(count, 1)
    pick = pl.pallas_call(
        pick_kernel,
        out_shape=jax.ShapeDtypeStruct((count, hypos * pats), BF16),
        in_specs=[in_vmem],
        out_specs=in_vmem,
        compiler_params=params,
        name="pick",
    )(combos)
    place = lax.axis_index(GROUP).astype(I32).reshape(1)
    parts = table_call(groups, samples, planes, hypos, pats, place, msg, pick)

    parts = lax.all_to_all(parts, PLANE, 0, 0, tiled=True)

    summed = pl.pallas_call(
        sum_kernel,
        out_shape=jax.ShapeDtypeStruct((count // planes, rows // 128, 128), F32),
        compiler_params=params,
        name="sum",
    )(parts)

    spectra = lax.all_to_all(summed, GROUP, 0, 0, tiled=True)

    tables = [jnp.asarray(t) for t in inverse_tables(groups, freqs, samples)]
    return pl.pallas_call(
        inverse_kernel,
        out_shape=jax.ShapeDtypeStruct((1, comps, samples), F32),
        compiler_params=params,
        name="inverse",
    )(spectra, *tables)


def solution(mesh):
    blk, sub = mesh.devices.shape
    fine = Mesh(mesh.devices.reshape(4, blk // 4, sub // 4, 2, 2), AXES)
    in_specs = (
        P(None, None, None, AXES, None),
        P(None, AXES),
        P(None, AXES),
        P(None, AXES),
        P(),
        P(),
    )
    out_specs = P(AXES, None, None)
    return jax.shard_map(on_device, mesh=fine, in_specs=in_specs, out_specs=out_specs, check_vma=False)
```

```python
import math

import jax
import jax.numpy as jnp
import ml_dtypes
import numpy as np
from jax import lax
from jax.experimental import pallas as pl
from jax.experimental.pallas import tpu as pltpu
from jax.sharding import Mesh
from jax.sharding import PartitionSpec as P

AXES = ("x", "zh", "y", "zl", "c")
GROUP = ("x", "c")
PLANE = ("zh", "y", "zl")
CODE_TOP = 32000.0
SLIP_UNIT = 2048.0
LEAST = 4e-34
F32, BF16, I32, I16 = jnp.float32, jnp.bfloat16, jnp.int32, jnp.int16
VMEM = 48 * 1024 * 1024
MERGE_VMEM = 63 * 1024 * 1024


def cos_sin(steps, samples):
    eighth = samples // 8
    quadrant = (steps + eighth) >> int(math.log2(samples // 4))
    rest = steps - quadrant * (samples // 4)
    t = rest.astype(F32) * (2.0 * math.pi / samples)
    t2 = t * t
    sine = t + t * t2 * (-1.0 / 6 + t2 * (1.0 / 120 + t2 * (-1.0 / 5040 + t2 * (1.0 / 362880))))
    cosine = 1.0 + t2 * (-0.5 + t2 * (1.0 / 24 + t2 * (-1.0 / 720 + t2 * (1.0 / 40320))))
    odd = (quadrant & 1) == 1
    c = jnp.where(odd, sine, cosine)
    s = jnp.where(odd, cosine, sine)
    c = jnp.where(((quadrant + 1) & 2) == 2, -c, c)
    s = jnp.where((quadrant & 2) == 2, -s, s)
    return c, s


def merge_kernel(groups, green_ref, mech_ref, slip_ref, onset_ref, out_ref, green, mech, slip, onset, merged, msg, sems, out_sems):
    _, comps, kinds, subs, freqs = green_ref.shape
    share = freqs // groups
    end = 2 * comps * share
    blocks = [(c, q) for c in range(comps) for q in range(2)]
    copies = [pltpu.make_async_copy(mech_ref, mech, sems.at[0])]
    for i, (c, q) in enumerate(blocks):
        copies.append(pltpu.make_async_copy(green_ref.at[q, c], green.at[i], sems.at[1 + i]))
    copies.append(pltpu.make_async_copy(slip_ref, slip, sems.at[1 + 2 * comps]))
    copies.append(pltpu.make_async_copy(onset_ref, onset, sems.at[2 + 2 * comps]))
    for copy in copies:
        copy.start()
    copies[0].wait()
    cols = [jnp.broadcast_to(mech[k : k + 1, :], (subs, subs)).T for k in range(kinds)]
    powers, sends = [], []
    for i in range(2 * comps):
        copies[1 + i].wait()
        top = jnp.zeros((8, subs), F32)
        for tile in range(freqs // subs):
            piece = slice(tile * subs, (tile + 1) * subs)
            total = cols[0] * green[i, 0, :, piece].astype(F32)
            for k in range(1, kinds):
                total = total + cols[k] * green[i, k, :, piece].astype(F32)
            total = total.T
            merged[i, piece, :] = total
            top = jnp.maximum(top, jnp.max(jnp.abs(total).reshape(subs // 8, 8, subs), axis=0))
        most = jnp.maximum(jnp.max(top, axis=0, keepdims=True), LEAST)
        power = jnp.maximum(jnp.ceil(jnp.log2(most * (1.0 / CODE_TOP))), -126.0)
        powers.append(power.astype(I32))
        inverse = jnp.exp2(-power)
        lines = slice(i * share, (i + 1) * share)
        for g in range(groups):
            part = merged[i, pl.ds(g, share, stride=groups), :] * inverse
            msg[g, lines, :] = jnp.round(part).astype(I32).astype(I16)
        sends.append(pltpu.make_async_copy(msg.at[:, lines], out_ref.at[:, lines], out_sems.at[i]))
        sends[-1].start()
        if i == 0:
            copies[-2].wait()
            codes = (slip[...].astype(F32) * SLIP_UNIT).astype(I32).astype(I16)
            for g in range(groups):
                msg[g, end + 16 :, :] = codes
            tail = slice(end + 16, msg.shape[1])
            sends.append(pltpu.make_async_copy(msg.at[:, tail], out_ref.at[:, tail], out_sems.at[2 * comps]))
            sends[-1].start()
    copies[-1].wait()
    head = jnp.concatenate([jnp.broadcast_to(p, (8 // len(powers), subs)) for p in powers] + [onset[...]], axis=0).astype(I16)
    for g in range(groups):
        msg[g, end : end + 16, :] = head
    sends.append(pltpu.make_async_copy(msg.at[:, end : end + 16], out_ref.at[:, end : end + 16], out_sems.at[2 * comps + 1]))
    sends[-1].start()
    for send in sends:
        send.wait()


def pick_kernel(combo_ref, pick_ref):
    count, entries = pick_ref.shape
    for first in range(0, entries, 128):
        ids = lax.broadcasted_iota(I32, (count, 128), 1) + first
        pick_ref[:, first : first + 128] = jnp.where(combo_ref[...] == ids, 1.0, 0.0).astype(BF16)


def table_kernel(groups, samples, place_ref, msg_ref, pick_ref, out_ref, slips, values, shifted, turns, table):
    hypos, _, rows = shifted.shape
    subs = values.shape[2]
    pats = slips.shape[0]
    share = rows // 4
    mine = place_ref[0]
    freq = mine + groups * lax.broadcasted_iota(I32, (8, subs), 0)

    for src in range(groups):
        lanes = slice(src * subs, (src + 1) * subs)
        slip = msg_ref[src, rows + 16 :, :].astype(I32).astype(F32) * (1.0 / SLIP_UNIT)
        slips[:, lanes] = slip.astype(BF16)
        head = msg_ref[src, rows : rows + 16, :].astype(I32)
        for i in range(4):
            lines = slice(i * share, (i + 1) * share)
            unit = jnp.exp2(head[2 * i : 2 * i + 1].astype(F32))
            values[src, lines, :] = msg_ref[src, lines, :].astype(I32).astype(F32) * unit
        near_c, near_s = cos_sin((head[8:16] * (8 * groups)) & (samples - 1), samples)
        turns[src, 0] = near_c
        turns[src, 1] = near_s
        turns[src, 2] = near_c * near_c - near_s * near_s
        turns[src, 3] = 2.0 * near_c * near_s

    spectra = None
    for h in range(hypos):
        for src in range(groups):
            lanes = slice(src * subs, (src + 1) * subs)
            onset = jnp.broadcast_to(msg_ref[src, rows : rows + 16, :].astype(I32)[8 + h : 9 + h], (8, subs))
            c0, s0 = cos_sin((onset * freq) & (samples - 1), samples)
            nc, ns = turns[src, 0, h : h + 1, :], turns[src, 1, h : h + 1, :]
            c = jnp.concatenate([c0, c0 * nc - s0 * ns], axis=0)
            s = jnp.concatenate([s0, s0 * nc + c0 * ns], axis=0)
            jc = jnp.broadcast_to(turns[src, 2, h : h + 1, :], (16, subs))
            js = jnp.broadcast_to(turns[src, 3, h : h + 1, :], (16, subs))
            real, imag = [[], []], [[], []]
            for a in range(share // 16):
                if a:
                    c, s = c * jc - s * js, s * jc + c * js
                for comp in range(2):
                    r0 = comp * 2 * share + a * 16
                    re = values[src, r0 : r0 + 16, :]
                    im = values[src, r0 + share : r0 + share + 16, :]
                    real[comp].append((c * re + s * im).astype(BF16))
                    imag[comp].append((c * im - s * re).astype(BF16))
            for comp in range(2):
                block = jnp.concatenate(real[comp] + imag[comp], axis=0).T
                shifted[h, lanes, comp * 2 * share : (comp + 1) * 2 * share] = block.astype(BF16)
        sums = jnp.dot(slips[...], shifted[h], preferred_element_type=F32)
        sums = sums.astype(BF16)
        table[h * pats : (h + 1) * pats, :] = sums
    spectra = jnp.dot(pick_ref[...], table[...], preferred_element_type=F32)
    dests = out_ref.shape[0]
    parts = [spectra[:, i : i + 128].reshape(dests, -1, 128) for i in range(0, rows, 128)]
    out_ref[...] = jnp.concatenate(parts, axis=1).astype(BF16)


def sum_kernel(in_ref, out_ref):
    total = jnp.sum(in_ref[...].astype(F32), axis=0)
    rows = out_ref.shape[0]
    for i in range(rows):
        for half in range(2):
            out_ref[i, half : half + 1, :] = total[half * rows + i : half * rows + i + 1, :]


def inverse_tables(groups, freqs, samples):
    share = freqs // groups
    k, b, g, a = np.arange(share), np.arange(128), np.arange(groups), np.arange(samples // 128)
    turn = 2.0 * math.pi / samples
    first = turn * (groups * k[:, None] * b[None, :] % samples)
    c, s = np.cos(first), np.sin(first)
    main = np.concatenate([np.concatenate([c, s], 1), np.concatenate([-s, c], 1)]) / math.sqrt(freqs)
    second = np.tile(turn * (g[:, None] * b[None, :] % samples), (2, 1))
    twist = np.stack([np.cos(second), np.sin(second)])
    third = turn * (128 * g[:, None] * a[None, :] % samples)
    last = np.stack([np.cos(third), -np.sin(third)])[..., None] * np.ones((1, 1, 1, 128))
    main = main.astype(np.float32)
    high = main.astype(ml_dtypes.bfloat16)
    low = (main - high.astype(np.float32)).astype(ml_dtypes.bfloat16)
    main = np.concatenate([high, low, high])
    return [main, twist.astype(np.float32), last.astype(np.float32)]


def inverse_kernel(in_ref, main_ref, twist_ref, last_ref, out_ref):
    groups, comps, width = in_ref.shape
    rows = jnp.concatenate([in_ref[:, comp, :] for comp in range(comps)], axis=0)
    row = lax.broadcasted_iota(I32, rows.shape, 0)
    lane = lax.broadcasted_iota(I32, rows.shape, 1)
    zero = (row % groups == 0) & (lane % (width // 2) == 0)
    rows = jnp.where(zero, 0.5 * rows, rows)
    high = rows.astype(BF16)
    low = (rows - high.astype(F32)).astype(BF16)
    v = jnp.dot(jnp.concatenate([high, high, low], axis=1), main_ref[...], preferred_element_type=F32)
    vr, vi = v[:, :128], v[:, 128:]
    c, s = twist_ref[0], twist_ref[1]
    ur, ui = vr * c - vi * s, vr * s + vi * c
    for comp in range(comps):
        total = None
        for g in range(groups):
            r = comp * groups + g
            term = last_ref[0, g] * ur[r : r + 1] + last_ref[1, g] * ui[r : r + 1]
            total = term if total is None else total + term
        for a in range(total.shape[0]):
            out_ref[0, comp : comp + 1, a * 128 : (a + 1) * 128] = total[a : a + 1]


def merge_call(groups, green, mechanism, slip, onset):
    _, comps, kinds, subs, freqs = green.shape
    pats, hypos = slip.shape[0], onset.shape[0]
    lines = 2 * comps * freqs // groups + 16 + pats
    return pl.pallas_call(
        lambda *refs: merge_kernel(groups, *refs),
        out_shape=jax.ShapeDtypeStruct((groups, lines, subs), I16),
        in_specs=[pl.BlockSpec(memory_space=pltpu.HBM)] * 4,
        out_specs=pl.BlockSpec(memory_space=pltpu.HBM),
        scratch_shapes=[
            pltpu.VMEM((2 * comps, kinds, subs, freqs), BF16),
            pltpu.VMEM((kinds, subs), F32),
            pltpu.VMEM((pats, subs), BF16),
            pltpu.VMEM((hypos, subs), I32),
            pltpu.VMEM((2 * comps, freqs, subs), F32),
            pltpu.VMEM((groups, lines, subs), I16),
            pltpu.SemaphoreType.DMA((2 * comps + 3,)),
            pltpu.SemaphoreType.DMA((2 * comps + 2,)),
        ],
        compiler_params=pltpu.CompilerParams(vmem_limit_bytes=MERGE_VMEM),
        name="merge",
    )(green, mechanism, slip, onset)


def table_call(groups, samples, planes, hypos, pats, place, msg, pick):
    subs = msg.shape[2]
    rows = msg.shape[1] - 16 - pats
    in_vmem = pl.BlockSpec(memory_space=pltpu.VMEM)
    return pl.pallas_call(
        lambda *refs: table_kernel(groups, samples, *refs),
        out_shape=jax.ShapeDtypeStruct((planes, pick.shape[0] // planes * (rows // 128), 128), BF16),
        in_specs=[pl.BlockSpec(memory_space=pltpu.SMEM), in_vmem, in_vmem],
        out_specs=in_vmem,
        scratch_shapes=[
            pltpu.VMEM((pats, groups * subs), BF16),
            pltpu.VMEM((groups, rows, subs), F32),
            pltpu.VMEM((hypos, groups * subs, rows), BF16),
            pltpu.VMEM((groups, 4, hypos, subs), F32),
            pltpu.VMEM((hypos * pats, rows), BF16),
        ],
        compiler_params=pltpu.CompilerParams(vmem_limit_bytes=VMEM),
        name="table",
    )(place, msg, pick)


def on_device(green, mechanism, slip, onset, pattern_of_variation, hypo_of_variation):
    _, comps, kinds, subs, freqs = green.shape
    samples = 2 * freqs
    pats, hypos = slip.shape[0], onset.shape[0]
    groups = lax.axis_size(GROUP)
    planes = lax.axis_size(PLANE)
    count = pattern_of_variation.shape[0]
    rows = 2 * comps * freqs // groups
    params = pltpu.CompilerParams(vmem_limit_bytes=VMEM)
    in_vmem = pl.BlockSpec(memory_space=pltpu.VMEM)

    msg = merge_call(groups, green, mechanism, slip, onset)
    msg = lax.all_to_all(msg, GROUP, 0, 0, tiled=True)

    combos = hypo_of_variation * pats + pattern_of_variation
    gx, gc = lax.axis_size("x"), lax.axis_size("c")
    combos = combos.reshape(gx, planes, gc).transpose(1, 0, 2).reshape(count, 1)
    pick = pl.pallas_call(
        pick_kernel,
        out_shape=jax.ShapeDtypeStruct((count, hypos * pats), BF16),
        in_specs=[in_vmem],
        out_specs=in_vmem,
        compiler_params=params,
        name="pick",
    )(combos)
    place = lax.axis_index(GROUP).astype(I32).reshape(1)
    parts = table_call(groups, samples, planes, hypos, pats, place, msg, pick)

    parts = lax.all_to_all(parts, PLANE, 0, 0, tiled=True)

    summed = pl.pallas_call(
        sum_kernel,
        out_shape=jax.ShapeDtypeStruct((count // planes, rows // 128, 128), F32),
        compiler_params=params,
        name="sum",
    )(parts)

    spectra = lax.all_to_all(summed, GROUP, 0, 0, tiled=True)

    tables = [jnp.asarray(t) for t in inverse_tables(groups, freqs, samples)]
    return pl.pallas_call(
        inverse_kernel,
        out_shape=jax.ShapeDtypeStruct((1, comps, samples), F32),
        compiler_params=params,
        name="inverse",
    )(spectra, *tables)


def solution(mesh):
    blk, sub = mesh.devices.shape
    fine = Mesh(mesh.devices.reshape(4, blk // 4, sub // 4, 2, 2), AXES)
    in_specs = (
        P(None, None, None, AXES, None),
        P(None, AXES),
        P(None, AXES),
        P(None, AXES),
        P(),
        P(),
    )
    out_specs = P(AXES, None, None)
    return jax.shard_map(on_device, mesh=fine, in_specs=in_specs, out_specs=out_specs, check_vma=False)
```

```python
import math

import jax
import jax.numpy as jnp
import ml_dtypes
import numpy as np
from jax import lax
from jax.experimental import pallas as pl
from jax.experimental.pallas import tpu as pltpu
from jax.sharding import Mesh
from jax.sharding import PartitionSpec as P

AXES = ("x", "zh", "y", "zl", "c")
GROUP = ("x", "c")
PLANE = ("zh", "y", "zl")
CODE_TOP = 32000.0
SLIP_UNIT = 2048.0
LEAST = 4e-34
F32, BF16, I32, I16 = jnp.float32, jnp.bfloat16, jnp.int32, jnp.int16
VMEM = 48 * 1024 * 1024


def cos_sin(steps, samples):
    eighth = samples // 8
    quadrant = (steps + eighth) >> int(math.log2(samples // 4))
    rest = steps - quadrant * (samples // 4)
    t = rest.astype(F32) * (2.0 * math.pi / samples)
    t2 = t * t
    sine = t + t * t2 * (-1.0 / 6 + t2 * (1.0 / 120 + t2 * (-1.0 / 5040)))
    cosine = 1.0 + t2 * (-0.5 + t2 * (1.0 / 24 + t2 * (-1.0 / 720)))
    odd = (quadrant & 1) == 1
    c = jnp.where(odd, sine, cosine)
    s = jnp.where(odd, cosine, sine)
    c = jnp.where(((quadrant + 1) & 2) == 2, -c, c)
    s = jnp.where((quadrant & 2) == 2, -s, s)
    return c, s


def merge_kernel(groups, green_ref, mech_ref, slip_ref, onset_ref, msg_ref, green, mech, slip, onset, merged, sems):
    _, comps, kinds, subs, freqs = green_ref.shape
    share = freqs // groups
    end = 2 * comps * share
    blocks = [(c, q) for c in range(comps) for q in range(2)]
    copies = [pltpu.make_async_copy(mech_ref, mech, sems.at[0])]
    for i, (c, q) in enumerate(blocks):
        copies.append(pltpu.make_async_copy(green_ref.at[q, c], green.at[i], sems.at[1 + i]))
    copies.append(pltpu.make_async_copy(slip_ref, slip, sems.at[1 + 2 * comps]))
    copies.append(pltpu.make_async_copy(onset_ref, onset, sems.at[2 + 2 * comps]))
    for copy in copies:
        copy.start()
    copies[0].wait()
    cols = [jnp.broadcast_to(mech[k : k + 1, :], (subs, subs)).T for k in range(kinds)]
    powers = []
    for i in range(2 * comps):
        copies[1 + i].wait()
        top = jnp.zeros((8, subs), F32)
        for tile in range(freqs // subs):
            piece = slice(tile * subs, (tile + 1) * subs)
            total = cols[0] * green[i, 0, :, piece].astype(F32)
            for k in range(1, kinds):
                total = total + cols[k] * green[i, k, :, piece].astype(F32)
            total = total.T
            merged[i, piece, :] = total
            top = jnp.maximum(top, jnp.max(jnp.abs(total).reshape(subs // 8, 8, subs), axis=0))
        most = jnp.maximum(jnp.max(top, axis=0, keepdims=True), LEAST)
        power = jnp.maximum(jnp.ceil(jnp.log2(most * (1.0 / CODE_TOP))), -126.0)
        powers.append(power.astype(I32))
        inverse = jnp.exp2(-power)
        lines = slice(i * share, (i + 1) * share)
        for g in range(groups):
            part = merged[i, pl.ds(g, share, stride=groups), :] * inverse
            msg_ref[g, lines, :] = jnp.round(part).astype(I32).astype(I16)
        if i == 0:
            copies[-2].wait()
            codes = (slip[...].astype(F32) * SLIP_UNIT).astype(I32).astype(I16)
            for g in range(groups):
                msg_ref[g, end + 16 :, :] = codes
    copies[-1].wait()
    head = jnp.concatenate([jnp.broadcast_to(p, (8 // len(powers), subs)) for p in powers] + [onset[...]], axis=0).astype(I16)
    for g in range(groups):
        msg_ref[g, end : end + 16, :] = head


def pick_kernel(combo_ref, pick_ref):
    count, entries = pick_ref.shape
    for first in range(0, entries, 128):
        ids = lax.broadcasted_iota(I32, (count, 128), 1) + first
        pick_ref[:, first : first + 128] = jnp.where(combo_ref[...] == ids, 1.0, 0.0).astype(BF16)


def table_kernel(groups, samples, place_ref, msg_ref, pick_ref, out_ref, slips, values, shifted, turns, table, onsets):
    hypos, _, rows = shifted.shape
    subs = values.shape[2]
    pats = slips.shape[0]
    share = rows // 4
    mine = place_ref[0]
    freq = mine + groups * lax.broadcasted_iota(I32, (8, subs), 0)

    for src in range(groups):
        lanes = slice(src * subs, (src + 1) * subs)
        slip = msg_ref[src, rows + 16 :, :].astype(I32).astype(F32) * (1.0 / SLIP_UNIT)
        slips[:, lanes] = slip.astype(BF16)
        head = msg_ref[src, rows : rows + 16, :].astype(I32)
        for i in range(4):
            lines = slice(i * share, (i + 1) * share)
            unit = jnp.exp2(head[2 * i : 2 * i + 1].astype(F32))
            values[src, lines, :] = msg_ref[src, lines, :].astype(I32).astype(F32) * unit
        onsets[src] = head[8:16]
        near_c, near_s = cos_sin((head[8:16] * (8 * groups)) & (samples - 1), samples)
        turns[src, 0] = near_c
        turns[src, 1] = near_s
        far_c, far_s = near_c * near_c - near_s * near_s, 2.0 * near_c * near_s
        twice_c, twice_s = far_c * far_c - far_s * far_s, 2.0 * far_c * far_s
        turns[src, 2], turns[src, 3] = far_c, far_s
        turns[src, 4], turns[src, 5] = twice_c, twice_s
        turns[src, 6], turns[src, 7] = far_c * twice_c - far_s * twice_s, far_c * twice_s + far_s * twice_c

    spectra = None
    batch = 2
    for h in range(hypos):
        for first in range(0, groups, batch):
            some = slice(first, first + batch)
            onset = jnp.concatenate([jnp.broadcast_to(onsets[src, h : h + 1, :], (8, subs)) for src in range(first, first + batch)], axis=0)
            c0, s0 = cos_sin((onset * jnp.concatenate([freq] * batch, axis=0)) & (samples - 1), samples)
            c0, s0 = c0.reshape(batch, 8, subs), s0.reshape(batch, 8, subs)

            def turned(pair, step):
                jc, js = turns[some, 2 * step, h : h + 1, :], turns[some, 2 * step + 1, h : h + 1, :]
                return pair[0] * jc - pair[1] * js, pair[1] * jc + pair[0] * js

            low = [(c0, s0), turned((c0, s0), 0)]
            real, imag = [[], []], [[], []]
            for a in range(share // 16):
                now = [turned(pair, a) for pair in low] if a else low
                for comp in range(2):
                    re_out, im_out = [], []
                    for half in range(2):
                        c, s = now[half]
                        r0 = comp * 2 * share + a * 16 + half * 8
                        re = values[some, r0 : r0 + 8, :]
                        im = values[some, r0 + share : r0 + share + 8, :]
                        re_out.append(c * re + s * im)
                        im_out.append(c * im - s * re)
                    real[comp].append(jnp.concatenate(re_out, axis=1).astype(BF16))
                    imag[comp].append(jnp.concatenate(im_out, axis=1).astype(BF16))
            for comp in range(2):
                block = jnp.concatenate(real[comp] + imag[comp], axis=1)
                for src in range(first, first + batch):
                    shifted[h, src * subs : (src + 1) * subs, comp * 2 * share : (comp + 1) * 2 * share] = block[src - first].T
        sums = jnp.dot(slips[...], shifted[h], preferred_element_type=F32)
        sums = sums.astype(BF16)
        table[h * pats : (h + 1) * pats, :] = sums
    spectra = jnp.dot(pick_ref[...], table[...], preferred_element_type=F32)
    dests = out_ref.shape[0]
    parts = [spectra[:, i : i + 128].reshape(dests, -1, 128) for i in range(0, rows, 128)]
    out_ref[...] = jnp.concatenate(parts, axis=1).astype(BF16)


def sum_kernel(in_ref, out_ref):
    total = jnp.sum(in_ref[...].astype(F32), axis=0)
    rows = out_ref.shape[0]
    for i in range(rows):
        for half in range(2):
            out_ref[i, half : half + 1, :] = total[half * rows + i : half * rows + i + 1, :]


def inverse_tables(groups, freqs, samples):
    share = freqs // groups
    k, b, g, a = np.arange(share), np.arange(128), np.arange(groups), np.arange(samples // 128)
    turn = 2.0 * math.pi / samples
    first = turn * (groups * k[:, None] * b[None, :] % samples)
    c, s = np.cos(first), np.sin(first)
    main = np.concatenate([np.concatenate([c, s], 1), np.concatenate([-s, c], 1)]) / math.sqrt(freqs)
    second = np.tile(turn * (g[:, None] * b[None, :] % samples), (2, 1))
    twist = np.stack([np.cos(second), np.sin(second)])
    third = turn * (128 * g[:, None] * a[None, :] % samples)
    last = np.stack([np.cos(third), -np.sin(third)])[..., None] * np.ones((1, 1, 1, 128))
    main = main.astype(np.float32)
    high = main.astype(ml_dtypes.bfloat16)
    low = (main - high.astype(np.float32)).astype(ml_dtypes.bfloat16)
    main = np.concatenate([high, low, high])
    return [main, twist.astype(np.float32), last.astype(np.float32)]


def inverse_kernel(in_ref, main_ref, twist_ref, last_ref, out_ref):
    groups, comps, width = in_ref.shape
    rows = jnp.concatenate([in_ref[:, comp, :] for comp in range(comps)], axis=0)
    row = lax.broadcasted_iota(I32, rows.shape, 0)
    lane = lax.broadcasted_iota(I32, rows.shape, 1)
    zero = (row % groups == 0) & (lane % (width // 2) == 0)
    rows = jnp.where(zero, 0.5 * rows, rows)
    high = rows.astype(BF16)
    low = (rows - high.astype(F32)).astype(BF16)
    v = jnp.dot(jnp.concatenate([high, high, low], axis=1), main_ref[...], preferred_element_type=F32)
    vr, vi = v[:, :128], v[:, 128:]
    c, s = twist_ref[0], twist_ref[1]
    ur, ui = vr * c - vi * s, vr * s + vi * c
    for comp in range(comps):
        total = None
        for g in range(groups):
            r = comp * groups + g
            term = last_ref[0, g] * ur[r : r + 1] + last_ref[1, g] * ui[r : r + 1]
            total = term if total is None else total + term
        for a in range(total.shape[0]):
            out_ref[0, comp : comp + 1, a * 128 : (a + 1) * 128] = total[a : a + 1]


def merge_call(groups, green, mechanism, slip, onset):
    _, comps, kinds, subs, freqs = green.shape
    pats, hypos = slip.shape[0], onset.shape[0]
    lines = 2 * comps * freqs // groups + 16 + pats
    return pl.pallas_call(
        lambda *refs: merge_kernel(groups, *refs),
        out_shape=jax.ShapeDtypeStruct((groups, lines, subs), I16),
        in_specs=[pl.BlockSpec(memory_space=pltpu.HBM)] * 4,
        out_specs=pl.BlockSpec(memory_space=pltpu.VMEM),
        scratch_shapes=[
            pltpu.VMEM((2 * comps, kinds, subs, freqs), BF16),
            pltpu.VMEM((kinds, subs), F32),
            pltpu.VMEM((pats, subs), BF16),
            pltpu.VMEM((hypos, subs), I32),
            pltpu.VMEM((2 * comps, freqs, subs), F32),
            pltpu.SemaphoreType.DMA((2 * comps + 3,)),
        ],
        compiler_params=pltpu.CompilerParams(vmem_limit_bytes=VMEM),
        name="merge",
    )(*(pltpu.with_memory_space_constraint(v, pltpu.HBM) for v in (green, mechanism, slip, onset)))


def table_call(groups, samples, planes, hypos, pats, place, msg, pick):
    subs = msg.shape[2]
    rows = msg.shape[1] - 16 - pats
    in_vmem = pl.BlockSpec(memory_space=pltpu.VMEM)
    return pl.pallas_call(
        lambda *refs: table_kernel(groups, samples, *refs),
        out_shape=jax.ShapeDtypeStruct((planes, pick.shape[0] // planes * (rows // 128), 128), BF16),
        in_specs=[pl.BlockSpec(memory_space=pltpu.SMEM), in_vmem, in_vmem],
        out_specs=in_vmem,
        scratch_shapes=[
            pltpu.VMEM((pats, groups * subs), BF16),
            pltpu.VMEM((groups, rows, subs), F32),
            pltpu.VMEM((hypos, groups * subs, rows), BF16),
            pltpu.VMEM((groups, 8, hypos, subs), F32),
            pltpu.VMEM((hypos * pats, rows), BF16),
            pltpu.VMEM((groups, hypos, subs), I32),
        ],
        compiler_params=pltpu.CompilerParams(vmem_limit_bytes=VMEM),
        name="table",
    )(place, msg, pick)


def on_device(green, mechanism, slip, onset, pattern_of_variation, hypo_of_variation):
    _, comps, kinds, subs, freqs = green.shape
    samples = 2 * freqs
    pats, hypos = slip.shape[0], onset.shape[0]
    groups = lax.axis_size(GROUP)
    planes = lax.axis_size(PLANE)
    count = pattern_of_variation.shape[0]
    rows = 2 * comps * freqs // groups
    params = pltpu.CompilerParams(vmem_limit_bytes=VMEM)
    in_vmem = pl.BlockSpec(memory_space=pltpu.VMEM)

    msg = merge_call(groups, green, mechanism, slip, onset)
    msg = lax.all_to_all(msg, GROUP, 0, 0, tiled=True)

    combos = hypo_of_variation * pats + pattern_of_variation
    gx, gc = lax.axis_size("x"), lax.axis_size("c")
    combos = combos.reshape(gx, planes, gc).transpose(1, 0, 2).reshape(count, 1)
    pick = pl.pallas_call(
        pick_kernel,
        out_shape=jax.ShapeDtypeStruct((count, hypos * pats), BF16),
        in_specs=[in_vmem],
        out_specs=in_vmem,
        compiler_params=params,
        name="pick",
    )(combos)
    place = lax.axis_index(GROUP).astype(I32).reshape(1)
    parts = table_call(groups, samples, planes, hypos, pats, place, msg, pick)

    parts = lax.all_to_all(parts, PLANE, 0, 0, tiled=True)

    summed = pl.pallas_call(
        sum_kernel,
        out_shape=jax.ShapeDtypeStruct((count // planes, rows // 128, 128), F32),
        compiler_params=params,
        name="sum",
    )(parts)

    spectra = lax.all_to_all(summed, GROUP, 0, 0, tiled=True)

    tables = [jnp.asarray(t) for t in inverse_tables(groups, freqs, samples)]
    return pl.pallas_call(
        inverse_kernel,
        out_shape=jax.ShapeDtypeStruct((1, comps, samples), F32),
        compiler_params=params,
        name="inverse",
    )(spectra, *tables)


def solution(mesh):
    blk, sub = mesh.devices.shape
    fine = Mesh(mesh.devices.reshape(4, blk // 4, sub // 4, 2, 2), AXES)
    in_specs = (
        P(None, None, None, AXES, None),
        P(None, AXES),
        P(None, AXES),
        P(None, AXES),
        P(),
        P(),
    )
    out_specs = P(AXES, None, None)
    return jax.shard_map(on_device, mesh=fine, in_specs=in_specs, out_specs=out_specs, check_vma=False)
```

```python
import math

import jax
import jax.numpy as jnp
import ml_dtypes
import numpy as np
from jax import lax
from jax.experimental import pallas as pl
from jax.experimental.pallas import tpu as pltpu
from jax.sharding import Mesh
from jax.sharding import PartitionSpec as P

AXES = ("x", "zh", "y", "zl", "c")
GROUP = ("x", "c")
PLANE = ("zh", "y", "zl")
CODE_TOP = 32000.0
SLIP_UNIT = 2048.0
LEAST = 4e-34
F32, BF16, I32, I16 = jnp.float32, jnp.bfloat16, jnp.int32, jnp.int16
VMEM = 48 * 1024 * 1024


def cos_sin(steps, samples):
    eighth = samples // 8
    quadrant = (steps + eighth) >> int(math.log2(samples // 4))
    rest = steps - quadrant * (samples // 4)
    t = rest.astype(F32) * (2.0 * math.pi / samples)
    t2 = t * t
    sine = t + t * t2 * (-1.0 / 6 + t2 * (1.0 / 120 + t2 * (-1.0 / 5040)))
    cosine = 1.0 + t2 * (-0.5 + t2 * (1.0 / 24 + t2 * (-1.0 / 720)))
    odd = (quadrant & 1) == 1
    c = jnp.where(odd, sine, cosine)
    s = jnp.where(odd, cosine, sine)
    c = jnp.where(((quadrant + 1) & 2) == 2, -c, c)
    s = jnp.where((quadrant & 2) == 2, -s, s)
    return c, s


def choose(groups, ring, pats, pattern, hypo, pick_ref, across, ordered):
    count, entries = pick_ref.shape
    pair = groups * ring // count
    width = min(count, 128)
    for first in range(0, count, width):
        some = slice(first, first + width)
        combo = hypo[some] * pats + pattern[some]
        across[some, :] = jnp.broadcast_to(combo.reshape(1, width), (128, width)).T
    for place in range(groups):
        source = pl.ds(place // pair * ring + place % pair, count // groups, stride=pair)
        ordered[pl.ds(place, count // groups, stride=groups), :] = across[source, :]
    for first in range(0, entries, 128):
        ids = lax.broadcasted_iota(I32, (count, 128), 1) + first
        pick_ref[:, first : first + 128] = jnp.where(ordered[...] == ids, 1.0, 0.0).astype(BF16)


def merge_kernel(groups, ring, pats, green_ref, mech_ref, slip_ref, onset_ref, pattern_ref, hypo_ref, msg_ref, pick_ref, green, mech, slip, onset, pattern, hypo, across, ordered, merged, sems):
    _, comps, kinds, subs, freqs = green_ref.shape
    share = freqs // groups
    end = 2 * comps * share
    blocks = [(c, q) for c in range(comps) for q in range(2)]
    copies = [pltpu.make_async_copy(mech_ref, mech, sems.at[0])]
    for i, (c, q) in enumerate(blocks):
        copies.append(pltpu.make_async_copy(green_ref.at[q, c], green.at[i], sems.at[1 + i]))
    copies.append(pltpu.make_async_copy(slip_ref, slip, sems.at[1 + 2 * comps]))
    copies.append(pltpu.make_async_copy(onset_ref, onset, sems.at[2 + 2 * comps]))
    rest = [
        pltpu.make_async_copy(pattern_ref, pattern, sems.at[3 + 2 * comps]),
        pltpu.make_async_copy(hypo_ref, hypo, sems.at[4 + 2 * comps]),
    ]
    for copy in rest + copies:
        copy.start()
    for copy in rest:
        copy.wait()
    choose(groups, ring, pats, pattern, hypo, pick_ref, across, ordered)
    copies[0].wait()
    cols = [jnp.broadcast_to(mech[k : k + 1, :], (subs, subs)).T for k in range(kinds)]
    powers = []
    for i in range(2 * comps):
        copies[1 + i].wait()
        top = jnp.zeros((8, subs), F32)
        for tile in range(freqs // subs):
            piece = slice(tile * subs, (tile + 1) * subs)
            total = cols[0] * green[i, 0, :, piece].astype(F32)
            for k in range(1, kinds):
                total = total + cols[k] * green[i, k, :, piece].astype(F32)
            total = total.T
            merged[i, piece, :] = total
            top = jnp.maximum(top, jnp.max(jnp.abs(total).reshape(subs // 8, 8, subs), axis=0))
        most = jnp.maximum(jnp.max(top, axis=0, keepdims=True), LEAST)
        power = jnp.maximum(jnp.ceil(jnp.log2(most * (1.0 / CODE_TOP))), -126.0)
        powers.append(power.astype(I32))
        inverse = jnp.exp2(-power)
        lines = slice(i * share, (i + 1) * share)
        for g in range(groups):
            part = merged[i, pl.ds(g, share, stride=groups), :] * inverse
            msg_ref[g, lines, :] = jnp.round(part).astype(I32).astype(I16)
        if i == 0:
            copies[-2].wait()
            codes = (slip[...].astype(F32) * SLIP_UNIT).astype(I32).astype(I16)
            for g in range(groups):
                msg_ref[g, end + 16 :, :] = codes
    copies[-1].wait()
    for g in range(groups):
        rows = powers + [jnp.full((8 - len(powers), subs), g, I32), onset[...]]
        msg_ref[g, end : end + 16, :] = jnp.concatenate(rows, axis=0).astype(I16)


def table_kernel(groups, samples, msg_ref, pick_ref, out_ref, slips, values, shifted, turns, table, onsets):
    hypos, _, rows = shifted.shape
    subs = values.shape[2]
    pats = slips.shape[0]
    share = rows // 4
    mine = msg_ref[0, rows : rows + 16, :].astype(I32)[4:5]
    freq = mine + groups * lax.broadcasted_iota(I32, (8, subs), 0)

    for src in range(groups):
        lanes = slice(src * subs, (src + 1) * subs)
        slip = msg_ref[src, rows + 16 :, :].astype(I32).astype(F32) * (1.0 / SLIP_UNIT)
        slips[:, lanes] = slip.astype(BF16)
        head = msg_ref[src, rows : rows + 16, :].astype(I32)
        for i in range(4):
            lines = slice(i * share, (i + 1) * share)
            unit = jnp.exp2(head[i : i + 1].astype(F32))
            values[src, lines, :] = msg_ref[src, lines, :].astype(I32).astype(F32) * unit
        onsets[src] = head[8:16]
        near_c, near_s = cos_sin((head[8:16] * (8 * groups)) & (samples - 1), samples)
        turns[src, 0] = near_c
        turns[src, 1] = near_s
        far_c, far_s = near_c * near_c - near_s * near_s, 2.0 * near_c * near_s
        twice_c, twice_s = far_c * far_c - far_s * far_s, 2.0 * far_c * far_s
        turns[src, 2], turns[src, 3] = far_c, far_s
        turns[src, 4], turns[src, 5] = twice_c, twice_s
        turns[src, 6], turns[src, 7] = far_c * twice_c - far_s * twice_s, far_c * twice_s + far_s * twice_c

    spectra = None
    batch = 2
    for h in range(hypos):
        for first in range(0, groups, batch):
            some = slice(first, first + batch)
            onset = jnp.concatenate([jnp.broadcast_to(onsets[src, h : h + 1, :], (8, subs)) for src in range(first, first + batch)], axis=0)
            c0, s0 = cos_sin((onset * jnp.concatenate([freq] * batch, axis=0)) & (samples - 1), samples)
            c0, s0 = c0.reshape(batch, 8, subs), s0.reshape(batch, 8, subs)

            def turned(pair, step):
                jc, js = turns[some, 2 * step, h : h + 1, :], turns[some, 2 * step + 1, h : h + 1, :]
                return pair[0] * jc - pair[1] * js, pair[1] * jc + pair[0] * js

            low = [(c0, s0), turned((c0, s0), 0)]
            real, imag = [[], []], [[], []]
            for a in range(share // 16):
                now = [turned(pair, a) for pair in low] if a else low
                for comp in range(2):
                    re_out, im_out = [], []
                    for half in range(2):
                        c, s = now[half]
                        r0 = comp * 2 * share + a * 16 + half * 8
                        re = values[some, r0 : r0 + 8, :]
                        im = values[some, r0 + share : r0 + share + 8, :]
                        re_out.append(c * re + s * im)
                        im_out.append(c * im - s * re)
                    real[comp].append(jnp.concatenate(re_out, axis=1).astype(BF16))
                    imag[comp].append(jnp.concatenate(im_out, axis=1).astype(BF16))
            for comp in range(2):
                block = jnp.concatenate(real[comp] + imag[comp], axis=1)
                for src in range(first, first + batch):
                    shifted[h, src * subs : (src + 1) * subs, comp * 2 * share : (comp + 1) * 2 * share] = block[src - first].T
        sums = jnp.dot(slips[...], shifted[h], preferred_element_type=F32)
        sums = sums.astype(BF16)
        table[h * pats : (h + 1) * pats, :] = sums
    spectra = jnp.dot(pick_ref[...], table[...], preferred_element_type=F32)
    dests = out_ref.shape[0]
    parts = [spectra[:, i : i + 128].reshape(dests, -1, 128) for i in range(0, rows, 128)]
    out_ref[...] = jnp.concatenate(parts, axis=1).astype(BF16)


def sum_kernel(in_ref, out_ref):
    total = jnp.sum(in_ref[...].astype(F32), axis=0)
    rows = out_ref.shape[0]
    for i in range(rows):
        for half in range(2):
            out_ref[i, half : half + 1, :] = total[half * rows + i : half * rows + i + 1, :]


def inverse_tables(groups, freqs, samples):
    share = freqs // groups
    k, b, g, a = np.arange(share), np.arange(128), np.arange(groups), np.arange(samples // 128)
    turn = 2.0 * math.pi / samples
    first = turn * (groups * k[:, None] * b[None, :] % samples)
    c, s = np.cos(first), np.sin(first)
    main = np.concatenate([np.concatenate([c, s], 1), np.concatenate([-s, c], 1)]) / math.sqrt(freqs)
    second = np.tile(turn * (g[:, None] * b[None, :] % samples), (2, 1))
    twist = np.stack([np.cos(second), np.sin(second)])
    third = turn * (128 * g[:, None] * a[None, :] % samples)
    last = np.stack([np.cos(third), -np.sin(third)])[..., None] * np.ones((1, 1, 1, 128))
    main = main.astype(np.float32)
    high = main.astype(ml_dtypes.bfloat16)
    low = (main - high.astype(np.float32)).astype(ml_dtypes.bfloat16)
    main = np.concatenate([high, low, high])
    return [main, twist.astype(np.float32), last.astype(np.float32)]


def inverse_kernel(in_ref, main_ref, twist_ref, last_ref, out_ref):
    groups, comps, width = in_ref.shape
    rows = jnp.concatenate([in_ref[:, comp, :] for comp in range(comps)], axis=0)
    row = lax.broadcasted_iota(I32, rows.shape, 0)
    lane = lax.broadcasted_iota(I32, rows.shape, 1)
    zero = (row % groups == 0) & (lane % (width // 2) == 0)
    rows = jnp.where(zero, 0.5 * rows, rows)
    high = rows.astype(BF16)
    low = (rows - high.astype(F32)).astype(BF16)
    v = jnp.dot(jnp.concatenate([high, high, low], axis=1), main_ref[...], preferred_element_type=F32)
    vr, vi = v[:, :128], v[:, 128:]
    c, s = twist_ref[0], twist_ref[1]
    ur, ui = vr * c - vi * s, vr * s + vi * c
    for comp in range(comps):
        total = None
        for g in range(groups):
            r = comp * groups + g
            term = last_ref[0, g] * ur[r : r + 1] + last_ref[1, g] * ui[r : r + 1]
            total = term if total is None else total + term
        for a in range(total.shape[0]):
            out_ref[0, comp : comp + 1, a * 128 : (a + 1) * 128] = total[a : a + 1]


def merge_call(groups, ring, green, mechanism, slip, onset, pattern, hypo):
    _, comps, kinds, subs, freqs = green.shape
    pats, hypos = slip.shape[0], onset.shape[0]
    lines = 2 * comps * freqs // groups + 16 + pats
    count = pattern.shape[0]
    return pl.pallas_call(
        lambda *refs: merge_kernel(groups, ring, pats, *refs),
        out_shape=(
            jax.ShapeDtypeStruct((groups, lines, subs), I16),
            jax.ShapeDtypeStruct((count, hypos * pats), BF16),
        ),
        in_specs=[pl.BlockSpec(memory_space=pltpu.HBM)] * 6,
        out_specs=(pl.BlockSpec(memory_space=pltpu.VMEM),) * 2,
        scratch_shapes=[
            pltpu.VMEM((2 * comps, kinds, subs, freqs), BF16),
            pltpu.VMEM((kinds, subs), F32),
            pltpu.VMEM((pats, subs), BF16),
            pltpu.VMEM((hypos, subs), I32),
            pltpu.VMEM((count,), I32),
            pltpu.VMEM((count,), I32),
            pltpu.VMEM((count, 128), I32),
            pltpu.VMEM((count, 128), I32),
            pltpu.VMEM((2 * comps, freqs, subs), F32),
            pltpu.SemaphoreType.DMA((2 * comps + 5,)),
        ],
        compiler_params=pltpu.CompilerParams(vmem_limit_bytes=VMEM),
        name="merge",
    )(*(pltpu.with_memory_space_constraint(v, pltpu.HBM) for v in (green, mechanism, slip, onset, pattern, hypo)))


def table_call(groups, samples, planes, hypos, pats, msg, pick):
    subs = msg.shape[2]
    rows = msg.shape[1] - 16 - pats
    in_vmem = pl.BlockSpec(memory_space=pltpu.VMEM)
    return pl.pallas_call(
        lambda *refs: table_kernel(groups, samples, *refs),
        out_shape=jax.ShapeDtypeStruct((planes, pick.shape[0] // planes * (rows // 128), 128), BF16),
        in_specs=[in_vmem, in_vmem],
        out_specs=in_vmem,
        scratch_shapes=[
            pltpu.VMEM((pats, groups * subs), BF16),
            pltpu.VMEM((groups, rows, subs), F32),
            pltpu.VMEM((hypos, groups * subs, rows), BF16),
            pltpu.VMEM((groups, 8, hypos, subs), F32),
            pltpu.VMEM((hypos * pats, rows), BF16),
            pltpu.VMEM((groups, hypos, subs), I32),
        ],
        compiler_params=pltpu.CompilerParams(vmem_limit_bytes=VMEM),
        name="table",
    )(msg, pick)


def on_device(green, mechanism, slip, onset, pattern_of_variation, hypo_of_variation):
    _, comps, kinds, subs, freqs = green.shape
    samples = 2 * freqs
    pats, hypos = slip.shape[0], onset.shape[0]
    groups = lax.axis_size(GROUP)
    planes = lax.axis_size(PLANE)
    count = pattern_of_variation.shape[0]
    rows = 2 * comps * freqs // groups
    params = pltpu.CompilerParams(vmem_limit_bytes=VMEM)

    ring = count // lax.axis_size("x")
    msg, pick = merge_call(groups, ring, green, mechanism, slip, onset, pattern_of_variation, hypo_of_variation)
    msg = lax.all_to_all(msg, GROUP, 0, 0, tiled=True)

    parts = table_call(groups, samples, planes, hypos, pats, msg, pick)

    parts = lax.all_to_all(parts, PLANE, 0, 0, tiled=True)

    summed = pl.pallas_call(
        sum_kernel,
        out_shape=jax.ShapeDtypeStruct((count // planes, rows // 128, 128), F32),
        compiler_params=params,
        name="sum",
    )(parts)

    spectra = lax.all_to_all(summed, GROUP, 0, 0, tiled=True)

    tables = [jnp.asarray(t) for t in inverse_tables(groups, freqs, samples)]
    return pl.pallas_call(
        inverse_kernel,
        out_shape=jax.ShapeDtypeStruct((1, comps, samples), F32),
        compiler_params=params,
        name="inverse",
    )(spectra, *tables)


def solution(mesh):
    blk, sub = mesh.devices.shape
    fine = Mesh(mesh.devices.reshape(4, blk // 4, sub // 4, 2, 2), AXES)
    in_specs = (
        P(None, None, None, AXES, None),
        P(None, AXES),
        P(None, AXES),
        P(None, AXES),
        P(),
        P(),
    )
    out_specs = P(AXES, None, None)
    return jax.shard_map(on_device, mesh=fine, in_specs=in_specs, out_specs=out_specs, check_vma=False)
```

```python
import math

import jax
import jax.numpy as jnp
import ml_dtypes
import numpy as np
from jax import lax
from jax.experimental import pallas as pl
from jax.experimental.pallas import tpu as pltpu
from jax.sharding import Mesh
from jax.sharding import PartitionSpec as P

AXES = ("x", "zh", "y", "zl", "c")
GROUP = ("x", "c")
PLANE = ("zh", "y", "zl")
CODE_TOP = 32000.0
SLIP_UNIT = 2048.0
LEAST = 4e-34
F32, BF16, I32, I16 = jnp.float32, jnp.bfloat16, jnp.int32, jnp.int16
VMEM = 48 * 1024 * 1024


def cos_sin(steps, samples):
    eighth = samples // 8
    quadrant = (steps + eighth) >> int(math.log2(samples // 4))
    rest = steps - quadrant * (samples // 4)
    t = rest.astype(F32) * (2.0 * math.pi / samples)
    t2 = t * t
    sine = t + t * t2 * (-1.0 / 6 + t2 * (1.0 / 120 + t2 * (-1.0 / 5040)))
    cosine = 1.0 + t2 * (-0.5 + t2 * (1.0 / 24 + t2 * (-1.0 / 720)))
    odd = (quadrant & 1) == 1
    c = jnp.where(odd, sine, cosine)
    s = jnp.where(odd, cosine, sine)
    c = jnp.where(((quadrant + 1) & 2) == 2, -c, c)
    s = jnp.where((quadrant & 2) == 2, -s, s)
    return c, s


def choose(groups, ring, pats, pattern, hypo, pick_ref, across, ordered):
    count, entries = pick_ref.shape
    pair = groups * ring // count
    width = min(count, 128)
    for first in range(0, count, width):
        some = slice(first, first + width)
        combo = hypo[some] * pats + pattern[some]
        across[some, :] = jnp.broadcast_to(combo.reshape(1, width), (128, width)).T
    for place in range(groups):
        source = pl.ds(place // pair * ring + place % pair, count // groups, stride=pair)
        ordered[pl.ds(place, count // groups, stride=groups), :] = across[source, :]
    for first in range(0, entries, 128):
        ids = lax.broadcasted_iota(I32, (count, 128), 1) + first
        pick_ref[:, first : first + 128] = jnp.where(ordered[...] == ids, 1.0, 0.0).astype(BF16)


def merge_kernel(groups, ring, pats, green_ref, mech_ref, slip_ref, onset_ref, pattern_ref, hypo_ref, msg_ref, pick_ref, green, mech, slip, onset, pattern, hypo, across, ordered, merged, sems):
    _, comps, kinds, subs, freqs = green_ref.shape
    share = freqs // groups
    end = 2 * comps * share
    blocks = [(c, q) for c in range(comps) for q in range(2)]
    copies = [pltpu.make_async_copy(mech_ref, mech, sems.at[0])]
    for i, (c, q) in enumerate(blocks):
        copies.append(pltpu.make_async_copy(green_ref.at[q, c], green.at[i], sems.at[1 + i]))
    copies.append(pltpu.make_async_copy(slip_ref, slip, sems.at[1 + 2 * comps]))
    copies.append(pltpu.make_async_copy(onset_ref, onset, sems.at[2 + 2 * comps]))
    rest = [
        pltpu.make_async_copy(pattern_ref, pattern, sems.at[3 + 2 * comps]),
        pltpu.make_async_copy(hypo_ref, hypo, sems.at[4 + 2 * comps]),
    ]
    for copy in rest + copies[:1] + copies[-2:] + copies[1:-2]:
        copy.start()
    for copy in rest:
        copy.wait()
    choose(groups, ring, pats, pattern, hypo, pick_ref, across, ordered)
    copies[-2].wait()
    codes = (slip[...].astype(F32) * SLIP_UNIT).astype(I32).astype(I16)
    for g in range(groups):
        msg_ref[g, end + 16 :, :] = codes
    copies[0].wait()
    cols = [jnp.broadcast_to(mech[k : k + 1, :], (subs, subs)).T for k in range(kinds)]
    powers = []

    def merge(i):
        top = jnp.zeros((8, subs), F32)
        for tile in range(freqs // subs):
            piece = slice(tile * subs, (tile + 1) * subs)
            total = cols[0] * green[i, 0, :, piece].astype(F32)
            for k in range(1, kinds):
                total = total + cols[k] * green[i, k, :, piece].astype(F32)
            total = total.T
            merged[i, piece, :] = total
            top = jnp.maximum(top, jnp.max(jnp.abs(total).reshape(subs // 8, 8, subs), axis=0))
        return top

    def encode(i, top):
        most = jnp.maximum(jnp.max(top, axis=0, keepdims=True), LEAST)
        power = jnp.maximum(jnp.ceil(jnp.log2(most * (1.0 / CODE_TOP))), -126.0)
        powers.append(power.astype(I32))
        inverse = jnp.exp2(-power)
        lines = slice(i * share, (i + 1) * share)
        for g in range(groups):
            part = merged[i, pl.ds(g, share, stride=groups), :] * inverse
            msg_ref[g, lines, :] = jnp.round(part).astype(I32).astype(I16)

    for i in range(2 * comps):
        copies[1 + i].wait()
        top = merge(i)
        if i:
            encode(i - 1, before)
        before = top
    encode(2 * comps - 1, before)
    copies[-1].wait()
    for g in range(groups):
        rows = powers + [jnp.full((8 - len(powers), subs), g, I32), onset[...]]
        msg_ref[g, end : end + 16, :] = jnp.concatenate(rows, axis=0).astype(I16)


def table_kernel(groups, samples, msg_ref, pick_ref, out_ref, slips, values, shifted, turns, table, onsets):
    hypos, _, rows = shifted.shape
    subs = values.shape[2]
    pats = slips.shape[0]
    share = rows // 4
    mine = msg_ref[0, rows : rows + 16, :].astype(I32)[4:5]
    freq = mine + groups * lax.broadcasted_iota(I32, (8, subs), 0)

    for src in range(groups):
        lanes = slice(src * subs, (src + 1) * subs)
        slip = msg_ref[src, rows + 16 :, :].astype(I32).astype(F32) * (1.0 / SLIP_UNIT)
        slips[:, lanes] = slip.astype(BF16)
        head = msg_ref[src, rows : rows + 16, :].astype(I32)
        for i in range(4):
            lines = slice(i * share, (i + 1) * share)
            unit = jnp.exp2(head[i : i + 1].astype(F32))
            values[src, lines, :] = msg_ref[src, lines, :].astype(I32).astype(F32) * unit
        onsets[src] = head[8:16]
        near_c, near_s = cos_sin((head[8:16] * (8 * groups)) & (samples - 1), samples)
        turns[src, 0] = near_c
        turns[src, 1] = near_s
        far_c, far_s = near_c * near_c - near_s * near_s, 2.0 * near_c * near_s
        twice_c, twice_s = far_c * far_c - far_s * far_s, 2.0 * far_c * far_s
        turns[src, 2], turns[src, 3] = far_c, far_s
        turns[src, 4], turns[src, 5] = twice_c, twice_s
        turns[src, 6], turns[src, 7] = far_c * twice_c - far_s * twice_s, far_c * twice_s + far_s * twice_c

    spectra = None
    batch = 2
    for h in range(hypos):
        for first in range(0, groups, batch):
            some = slice(first, first + batch)
            onset = jnp.concatenate([jnp.broadcast_to(onsets[src, h : h + 1, :], (8, subs)) for src in range(first, first + batch)], axis=0)
            c0, s0 = cos_sin((onset * jnp.concatenate([freq] * batch, axis=0)) & (samples - 1), samples)
            c0, s0 = c0.reshape(batch, 8, subs), s0.reshape(batch, 8, subs)

            def turned(pair, step):
                jc, js = turns[some, 2 * step, h : h + 1, :], turns[some, 2 * step + 1, h : h + 1, :]
                return pair[0] * jc - pair[1] * js, pair[1] * jc + pair[0] * js

            low = [(c0, s0), turned((c0, s0), 0)]
            real, imag = [[], []], [[], []]
            for a in range(share // 16):
                now = [turned(pair, a) for pair in low] if a else low
                for comp in range(2):
                    re_out, im_out = [], []
                    for half in range(2):
                        c, s = now[half]
                        r0 = comp * 2 * share + a * 16 + half * 8
                        re = values[some, r0 : r0 + 8, :]
                        im = values[some, r0 + share : r0 + share + 8, :]
                        re_out.append(c * re + s * im)
                        im_out.append(c * im - s * re)
                    real[comp].append(jnp.concatenate(re_out, axis=1).astype(BF16))
                    imag[comp].append(jnp.concatenate(im_out, axis=1).astype(BF16))
            for comp in range(2):
                block = jnp.concatenate(real[comp] + imag[comp], axis=1)
                for src in range(first, first + batch):
                    shifted[h, src * subs : (src + 1) * subs, comp * 2 * share : (comp + 1) * 2 * share] = block[src - first].T
        sums = jnp.dot(slips[...], shifted[h], preferred_element_type=F32)
        sums = sums.astype(BF16)
        table[h * pats : (h + 1) * pats, :] = sums
    spectra = jnp.dot(pick_ref[...], table[...], preferred_element_type=F32)
    dests = out_ref.shape[0]
    parts = [spectra[:, i : i + 128].reshape(dests, -1, 128) for i in range(0, rows, 128)]
    out_ref[...] = jnp.concatenate(parts, axis=1).astype(BF16)


def sum_kernel(in_ref, out_ref):
    total = jnp.sum(in_ref[...].astype(F32), axis=0)
    rows = out_ref.shape[0]
    for i in range(rows):
        for half in range(2):
            out_ref[i, half : half + 1, :] = total[half * rows + i : half * rows + i + 1, :]


def inverse_tables(groups, freqs, samples):
    share = freqs // groups
    k, b, g, a = np.arange(share), np.arange(128), np.arange(groups), np.arange(samples // 128)
    turn = 2.0 * math.pi / samples
    first = turn * (groups * k[:, None] * b[None, :] % samples)
    c, s = np.cos(first), np.sin(first)
    main = np.concatenate([np.concatenate([c, s], 1), np.concatenate([-s, c], 1)]) / math.sqrt(freqs)
    second = np.tile(turn * (g[:, None] * b[None, :] % samples), (2, 1))
    twist = np.stack([np.cos(second), np.sin(second)])
    third = turn * (128 * g[:, None] * a[None, :] % samples)
    last = np.stack([np.cos(third), -np.sin(third)])[..., None] * np.ones((1, 1, 1, 128))
    main = main.astype(np.float32)
    high = main.astype(ml_dtypes.bfloat16)
    low = (main - high.astype(np.float32)).astype(ml_dtypes.bfloat16)
    main = np.concatenate([high, low, high])
    return [main, twist.astype(np.float32), last.astype(np.float32)]


def inverse_kernel(in_ref, main_ref, twist_ref, last_ref, out_ref):
    groups, comps, width = in_ref.shape
    rows = jnp.concatenate([in_ref[:, comp, :] for comp in range(comps)], axis=0)
    row = lax.broadcasted_iota(I32, rows.shape, 0)
    lane = lax.broadcasted_iota(I32, rows.shape, 1)
    zero = (row % groups == 0) & (lane % (width // 2) == 0)
    rows = jnp.where(zero, 0.5 * rows, rows)
    high = rows.astype(BF16)
    low = (rows - high.astype(F32)).astype(BF16)
    v = jnp.dot(jnp.concatenate([high, high, low], axis=1), main_ref[...], preferred_element_type=F32)
    vr, vi = v[:, :128], v[:, 128:]
    c, s = twist_ref[0], twist_ref[1]
    ur, ui = vr * c - vi * s, vr * s + vi * c
    for comp in range(comps):
        total = None
        for g in range(groups):
            r = comp * groups + g
            term = last_ref[0, g] * ur[r : r + 1] + last_ref[1, g] * ui[r : r + 1]
            total = term if total is None else total + term
        for a in range(total.shape[0]):
            out_ref[0, comp : comp + 1, a * 128 : (a + 1) * 128] = total[a : a + 1]


def merge_call(groups, ring, green, mechanism, slip, onset, pattern, hypo):
    _, comps, kinds, subs, freqs = green.shape
    pats, hypos = slip.shape[0], onset.shape[0]
    lines = 2 * comps * freqs // groups + 16 + pats
    count = pattern.shape[0]
    return pl.pallas_call(
        lambda *refs: merge_kernel(groups, ring, pats, *refs),
        out_shape=(
            jax.ShapeDtypeStruct((groups, lines, subs), I16),
            jax.ShapeDtypeStruct((count, hypos * pats), BF16),
        ),
        in_specs=[pl.BlockSpec(memory_space=pltpu.HBM)] * 6,
        out_specs=(pl.BlockSpec(memory_space=pltpu.VMEM),) * 2,
        scratch_shapes=[
            pltpu.VMEM((2 * comps, kinds, subs, freqs), BF16),
            pltpu.VMEM((kinds, subs), F32),
            pltpu.VMEM((pats, subs), BF16),
            pltpu.VMEM((hypos, subs), I32),
            pltpu.VMEM((count,), I32),
            pltpu.VMEM((count,), I32),
            pltpu.VMEM((count, 128), I32),
            pltpu.VMEM((count, 128), I32),
            pltpu.VMEM((2 * comps, freqs, subs), F32),
            pltpu.SemaphoreType.DMA((2 * comps + 5,)),
        ],
        compiler_params=pltpu.CompilerParams(vmem_limit_bytes=VMEM),
        name="merge",
    )(*(pltpu.with_memory_space_constraint(v, pltpu.HBM) for v in (green, mechanism, slip, onset, pattern, hypo)))


def table_call(groups, samples, planes, hypos, pats, msg, pick):
    subs = msg.shape[2]
    rows = msg.shape[1] - 16 - pats
    in_vmem = pl.BlockSpec(memory_space=pltpu.VMEM)
    return pl.pallas_call(
        lambda *refs: table_kernel(groups, samples, *refs),
        out_shape=jax.ShapeDtypeStruct((planes, pick.shape[0] // planes * (rows // 128), 128), BF16),
        in_specs=[in_vmem, in_vmem],
        out_specs=in_vmem,
        scratch_shapes=[
            pltpu.VMEM((pats, groups * subs), BF16),
            pltpu.VMEM((groups, rows, subs), F32),
            pltpu.VMEM((hypos, groups * subs, rows), BF16),
            pltpu.VMEM((groups, 8, hypos, subs), F32),
            pltpu.VMEM((hypos * pats, rows), BF16),
            pltpu.VMEM((groups, hypos, subs), I32),
        ],
        compiler_params=pltpu.CompilerParams(vmem_limit_bytes=VMEM),
        name="table",
    )(msg, pick)


def on_device(green, mechanism, slip, onset, pattern_of_variation, hypo_of_variation):
    _, comps, kinds, subs, freqs = green.shape
    samples = 2 * freqs
    pats, hypos = slip.shape[0], onset.shape[0]
    groups = lax.axis_size(GROUP)
    planes = lax.axis_size(PLANE)
    count = pattern_of_variation.shape[0]
    rows = 2 * comps * freqs // groups
    params = pltpu.CompilerParams(vmem_limit_bytes=VMEM)

    ring = count // lax.axis_size("x")
    msg, pick = merge_call(groups, ring, green, mechanism, slip, onset, pattern_of_variation, hypo_of_variation)
    msg = lax.all_to_all(msg, GROUP, 0, 0, tiled=True)

    parts = table_call(groups, samples, planes, hypos, pats, msg, pick)

    parts = lax.all_to_all(parts, PLANE, 0, 0, tiled=True)

    summed = pl.pallas_call(
        sum_kernel,
        out_shape=jax.ShapeDtypeStruct((count // planes, rows // 128, 128), F32),
        compiler_params=params,
        name="sum",
    )(parts)

    spectra = lax.all_to_all(summed, GROUP, 0, 0, tiled=True)

    tables = [jnp.asarray(t) for t in inverse_tables(groups, freqs, samples)]
    return pl.pallas_call(
        inverse_kernel,
        out_shape=jax.ShapeDtypeStruct((1, comps, samples), F32),
        compiler_params=params,
        name="inverse",
    )(spectra, *tables)


def solution(mesh):
    blk, sub = mesh.devices.shape
    fine = Mesh(mesh.devices.reshape(4, blk // 4, sub // 4, 2, 2), AXES)
    in_specs = (
        P(None, None, None, AXES, None),
        P(None, AXES),
        P(None, AXES),
        P(None, AXES),
        P(),
        P(),
    )
    out_specs = P(AXES, None, None)
    return jax.shard_map(on_device, mesh=fine, in_specs=in_specs, out_specs=out_specs, check_vma=False)
```

```python
import math

import jax
import jax.numpy as jnp
import ml_dtypes
import numpy as np
from jax import lax
from jax.experimental import pallas as pl
from jax.experimental.pallas import tpu as pltpu
from jax.sharding import Mesh
from jax.sharding import PartitionSpec as P

AXES = ("x", "zh", "y", "zl", "c")
GROUP = ("x", "c")
CODE_TOP = 32000.0
SLIP_UNIT = 2048.0
LEAST = 4e-34
F32, BF16, I32, I16 = jnp.float32, jnp.bfloat16, jnp.int32, jnp.int16
VMEM = 48 * 1024 * 1024


def cos_sin(steps, samples):
    eighth = samples // 8
    quadrant = (steps + eighth) >> int(math.log2(samples // 4))
    rest = steps - quadrant * (samples // 4)
    t = rest.astype(F32) * (2.0 * math.pi / samples)
    t2 = t * t
    sine = t + t * t2 * (-1.0 / 6 + t2 * (1.0 / 120 + t2 * (-1.0 / 5040)))
    cosine = 1.0 + t2 * (-0.5 + t2 * (1.0 / 24 + t2 * (-1.0 / 720)))
    odd = (quadrant & 1) == 1
    c = jnp.where(odd, sine, cosine)
    s = jnp.where(odd, cosine, sine)
    c = jnp.where(((quadrant + 1) & 2) == 2, -c, c)
    s = jnp.where((quadrant & 2) == 2, -s, s)
    return c, s


def choose(pats, pattern, hypo, pick_ref, across):
    count, entries = pick_ref.shape
    width = min(count, 128)
    for first in range(0, count, width):
        some = slice(first, first + width)
        combo = hypo[some] * pats + pattern[some]
        across[some, :] = jnp.broadcast_to(combo.reshape(1, width), (128, width)).T
    for first in range(0, entries, 128):
        ids = lax.broadcasted_iota(I32, (count, 128), 1) + first
        pick_ref[:, first : first + 128] = jnp.where(across[...] == ids, 1.0, 0.0).astype(BF16)


def merge_kernel(groups, pats, green_ref, mech_ref, slip_ref, onset_ref, pattern_ref, hypo_ref, msg_ref, pick_ref, green, mech, slip, onset, pattern, hypo, across, merged, sems):
    _, comps, kinds, subs, freqs = green_ref.shape
    share = freqs // groups
    end = 2 * comps * share
    blocks = [(c, q) for c in range(comps) for q in range(2)]
    copies = [pltpu.make_async_copy(mech_ref, mech, sems.at[0])]
    for i, (c, q) in enumerate(blocks):
        copies.append(pltpu.make_async_copy(green_ref.at[q, c], green.at[i], sems.at[1 + i]))
    copies.append(pltpu.make_async_copy(slip_ref, slip, sems.at[1 + 2 * comps]))
    copies.append(pltpu.make_async_copy(onset_ref, onset, sems.at[2 + 2 * comps]))
    rest = [
        pltpu.make_async_copy(pattern_ref, pattern, sems.at[3 + 2 * comps]),
        pltpu.make_async_copy(hypo_ref, hypo, sems.at[4 + 2 * comps]),
    ]
    for copy in rest + copies[:1] + copies[-2:] + copies[1:-2]:
        copy.start()
    for copy in rest:
        copy.wait()
    choose(pats, pattern, hypo, pick_ref, across)
    copies[-2].wait()
    codes = (slip[...].astype(F32) * SLIP_UNIT).astype(I32).astype(I16)
    for g in range(groups):
        msg_ref[g, end + 16 :, :] = codes
    copies[0].wait()
    cols = [jnp.broadcast_to(mech[k : k + 1, :], (subs, subs)).T for k in range(kinds)]
    powers = []

    def merge(i):
        top = jnp.zeros((8, subs), F32)
        for tile in range(freqs // subs):
            piece = slice(tile * subs, (tile + 1) * subs)
            total = cols[0] * green[i, 0, :, piece].astype(F32)
            for k in range(1, kinds):
                total = total + cols[k] * green[i, k, :, piece].astype(F32)
            total = total.T
            merged[i, piece, :] = total
            top = jnp.maximum(top, jnp.max(jnp.abs(total).reshape(subs // 8, 8, subs), axis=0))
        return top

    def encode(i, top):
        most = jnp.maximum(jnp.max(top, axis=0, keepdims=True), LEAST)
        power = jnp.maximum(jnp.ceil(jnp.log2(most * (1.0 / CODE_TOP))), -126.0)
        powers.append(power.astype(I32))
        inverse = jnp.exp2(-power)
        lines = slice(i * share, (i + 1) * share)
        for g in range(groups):
            part = merged[i, pl.ds(g, share, stride=groups), :] * inverse
            msg_ref[g, lines, :] = jnp.round(part).astype(I32).astype(I16)

    for i in range(2 * comps):
        copies[1 + i].wait()
        top = merge(i)
        if i:
            encode(i - 1, before)
        before = top
    encode(2 * comps - 1, before)
    copies[-1].wait()
    for g in range(groups):
        rows = powers + [jnp.full((8 - len(powers), subs), g, I32), onset[...]]
        msg_ref[g, end : end + 16, :] = jnp.concatenate(rows, axis=0).astype(I16)


def table_kernel(groups, samples, msg_ref, pick_ref, out_ref, slips, values, shifted, turns, table, onsets):
    hypos, _, rows = shifted.shape
    subs = values.shape[2]
    pats = slips.shape[0]
    share = rows // 4
    mine = msg_ref[0, rows : rows + 16, :].astype(I32)[4:5]
    freq = mine + groups * lax.broadcasted_iota(I32, (8, subs), 0)

    for src in range(groups):
        lanes = slice(src * subs, (src + 1) * subs)
        slip = msg_ref[src, rows + 16 :, :].astype(I32).astype(F32) * (1.0 / SLIP_UNIT)
        slips[:, lanes] = slip.astype(BF16)
        head = msg_ref[src, rows : rows + 16, :].astype(I32)
        for i in range(4):
            lines = slice(i * share, (i + 1) * share)
            unit = jnp.exp2(head[i : i + 1].astype(F32))
            values[src, lines, :] = msg_ref[src, lines, :].astype(I32).astype(F32) * unit
        onsets[src] = head[8:16]
        near_c, near_s = cos_sin((head[8:16] * (8 * groups)) & (samples - 1), samples)
        turns[src, 0] = near_c
        turns[src, 1] = near_s
        far_c, far_s = near_c * near_c - near_s * near_s, 2.0 * near_c * near_s
        twice_c, twice_s = far_c * far_c - far_s * far_s, 2.0 * far_c * far_s
        turns[src, 2], turns[src, 3] = far_c, far_s
        turns[src, 4], turns[src, 5] = twice_c, twice_s
        turns[src, 6], turns[src, 7] = far_c * twice_c - far_s * twice_s, far_c * twice_s + far_s * twice_c

    spectra = None
    batch = 2
    for h in range(hypos):
        for first in range(0, groups, batch):
            some = slice(first, first + batch)
            onset = jnp.concatenate([jnp.broadcast_to(onsets[src, h : h + 1, :], (8, subs)) for src in range(first, first + batch)], axis=0)
            c0, s0 = cos_sin((onset * jnp.concatenate([freq] * batch, axis=0)) & (samples - 1), samples)
            c0, s0 = c0.reshape(batch, 8, subs), s0.reshape(batch, 8, subs)

            def turned(pair, step):
                jc, js = turns[some, 2 * step, h : h + 1, :], turns[some, 2 * step + 1, h : h + 1, :]
                return pair[0] * jc - pair[1] * js, pair[1] * jc + pair[0] * js

            low = [(c0, s0), turned((c0, s0), 0)]
            real, imag = [[], []], [[], []]
            for a in range(share // 16):
                now = [turned(pair, a) for pair in low] if a else low
                for comp in range(2):
                    re_out, im_out = [], []
                    for half in range(2):
                        c, s = now[half]
                        r0 = comp * 2 * share + a * 16 + half * 8
                        re = values[some, r0 : r0 + 8, :]
                        im = values[some, r0 + share : r0 + share + 8, :]
                        re_out.append(c * re + s * im)
                        im_out.append(c * im - s * re)
                    real[comp].append(jnp.concatenate(re_out, axis=1).astype(BF16))
                    imag[comp].append(jnp.concatenate(im_out, axis=1).astype(BF16))
            for comp in range(2):
                block = jnp.concatenate(real[comp] + imag[comp], axis=1)
                for src in range(first, first + batch):
                    shifted[h, src * subs : (src + 1) * subs, comp * 2 * share : (comp + 1) * 2 * share] = block[src - first].T
        sums = jnp.dot(slips[...], shifted[h], preferred_element_type=F32)
        sums = sums.astype(BF16)
        table[h * pats : (h + 1) * pats, :] = sums
    spectra = jnp.dot(pick_ref[...], table[...], preferred_element_type=F32)
    out_ref[...] = spectra.reshape(out_ref.shape).astype(BF16)


def inverse_tables(groups, freqs, samples):
    share = freqs // groups
    k, b, g, a = np.arange(share), np.arange(128), np.arange(groups), np.arange(samples // 128)
    turn = 2.0 * math.pi / samples
    first = turn * (groups * k[:, None] * b[None, :] % samples)
    c, s = np.cos(first), np.sin(first)
    main = np.concatenate([np.concatenate([c, s], 1), np.concatenate([-s, c], 1)]) / math.sqrt(freqs)
    second = np.tile(turn * (g[:, None] * b[None, :] % samples), (2, 1))
    twist = np.stack([np.cos(second), np.sin(second)])
    third = turn * (128 * g[:, None] * a[None, :] % samples)
    last = np.stack([np.cos(third), -np.sin(third)])[..., None] * np.ones((1, 1, 1, 128))
    main = main.astype(np.float32)
    high = main.astype(ml_dtypes.bfloat16)
    low = (main - high.astype(np.float32)).astype(ml_dtypes.bfloat16)
    main = np.concatenate([high, low, high])
    return [main, twist.astype(np.float32), last.astype(np.float32)]


def inverse_kernel(rings, pair, in_ref, main_ref, twist_ref, last_ref, out_ref):
    count, comps, width = in_ref.shape
    groups = rings * pair
    ring = count // rings
    sums = []
    for x in range(rings):
        part = in_ref[x * ring : (x + 1) * ring].astype(F32).reshape(ring // pair, pair * comps, width)
        sums.append(jnp.sum(part, axis=0))
    sums = jnp.concatenate(sums, axis=0)
    rows = jnp.concatenate([sums[i : i + 1] for comp in range(comps) for i in range(comp, groups * comps, comps)], axis=0)
    row = lax.broadcasted_iota(I32, rows.shape, 0)
    lane = lax.broadcasted_iota(I32, rows.shape, 1)
    zero = (row % groups == 0) & (lane % (width // 2) == 0)
    rows = jnp.where(zero, 0.5 * rows, rows)
    high = rows.astype(BF16)
    low = (rows - high.astype(F32)).astype(BF16)
    v = jnp.dot(jnp.concatenate([high, high, low], axis=1), main_ref[...], preferred_element_type=F32)
    vr, vi = v[:, :128], v[:, 128:]
    c, s = twist_ref[0], twist_ref[1]
    ur, ui = vr * c - vi * s, vr * s + vi * c
    for comp in range(comps):
        total = None
        for g in range(groups):
            r = comp * groups + g
            term = last_ref[0, g] * ur[r : r + 1] + last_ref[1, g] * ui[r : r + 1]
            total = term if total is None else total + term
        for a in range(total.shape[0]):
            out_ref[0, comp : comp + 1, a * 128 : (a + 1) * 128] = total[a : a + 1]


def merge_call(groups, green, mechanism, slip, onset, pattern, hypo):
    _, comps, kinds, subs, freqs = green.shape
    pats, hypos = slip.shape[0], onset.shape[0]
    lines = 2 * comps * freqs // groups + 16 + pats
    count = pattern.shape[0]
    return pl.pallas_call(
        lambda *refs: merge_kernel(groups, pats, *refs),
        out_shape=(
            jax.ShapeDtypeStruct((groups, lines, subs), I16),
            jax.ShapeDtypeStruct((count, hypos * pats), BF16),
        ),
        in_specs=[pl.BlockSpec(memory_space=pltpu.HBM)] * 6,
        out_specs=(pl.BlockSpec(memory_space=pltpu.VMEM),) * 2,
        scratch_shapes=[
            pltpu.VMEM((2 * comps, kinds, subs, freqs), BF16),
            pltpu.VMEM((kinds, subs), F32),
            pltpu.VMEM((pats, subs), BF16),
            pltpu.VMEM((hypos, subs), I32),
            pltpu.VMEM((count,), I32),
            pltpu.VMEM((count,), I32),
            pltpu.VMEM((count, 128), I32),
            pltpu.VMEM((2 * comps, freqs, subs), F32),
            pltpu.SemaphoreType.DMA((2 * comps + 5,)),
        ],
        compiler_params=pltpu.CompilerParams(vmem_limit_bytes=VMEM),
        name="merge",
    )(*(pltpu.with_memory_space_constraint(v, pltpu.HBM) for v in (green, mechanism, slip, onset, pattern, hypo)))


def table_call(groups, samples, hypos, pats, msg, pick):
    subs = msg.shape[2]
    rows = msg.shape[1] - 16 - pats
    in_vmem = pl.BlockSpec(memory_space=pltpu.VMEM)
    return pl.pallas_call(
        lambda *refs: table_kernel(groups, samples, *refs),
        out_shape=jax.ShapeDtypeStruct((pick.shape[0], rows // 128, 128), BF16),
        in_specs=[in_vmem, in_vmem],
        out_specs=in_vmem,
        scratch_shapes=[
            pltpu.VMEM((pats, groups * subs), BF16),
            pltpu.VMEM((groups, rows, subs), F32),
            pltpu.VMEM((hypos, groups * subs, rows), BF16),
            pltpu.VMEM((groups, 8, hypos, subs), F32),
            pltpu.VMEM((hypos * pats, rows), BF16),
            pltpu.VMEM((groups, hypos, subs), I32),
        ],
        compiler_params=pltpu.CompilerParams(vmem_limit_bytes=VMEM),
        name="table",
    )(msg, pick)


def on_device(green, mechanism, slip, onset, pattern_of_variation, hypo_of_variation):
    _, comps, kinds, subs, freqs = green.shape
    samples = 2 * freqs
    pats, hypos = slip.shape[0], onset.shape[0]
    groups = lax.axis_size(GROUP)
    params = pltpu.CompilerParams(vmem_limit_bytes=VMEM)

    msg, pick = merge_call(groups, green, mechanism, slip, onset, pattern_of_variation, hypo_of_variation)
    msg = lax.all_to_all(msg, GROUP, 0, 0, tiled=True)
    parts = table_call(groups, samples, hypos, pats, msg, pick)
    parts = lax.all_to_all(parts, AXES, 0, 0, tiled=True)

    tables = [jnp.asarray(t) for t in inverse_tables(groups, freqs, samples)]
    return pl.pallas_call(
        lambda *refs: inverse_kernel(lax.axis_size("x"), lax.axis_size("c"), *refs),
        out_shape=jax.ShapeDtypeStruct((1, comps, samples), F32),
        compiler_params=params,
        name="inverse",
    )(parts, *tables)


def solution(mesh):
    blk, sub = mesh.devices.shape
    fine = Mesh(mesh.devices.reshape(4, blk // 4, sub // 4, 2, 2), AXES)
    in_specs = (
        P(None, None, None, AXES, None),
        P(None, AXES),
        P(None, AXES),
        P(None, AXES),
        P(),
        P(),
    )
    out_specs = P(AXES, None, None)
    return jax.shard_map(on_device, mesh=fine, in_specs=in_specs, out_specs=out_specs, check_vma=False)
```

```python
import math

import jax
import jax.numpy as jnp
import ml_dtypes
import numpy as np
from jax import lax
from jax.experimental import pallas as pl
from jax.experimental.pallas import tpu as pltpu
from jax.sharding import Mesh
from jax.sharding import PartitionSpec as P

AXES = ("x", "zh", "y", "zl", "c")
GROUP = ("c", "x")
OWNERS = AXES[::-1]
CODE_TOP = 32000.0
SLIP_UNIT = 2048.0
LEAST = 4e-34
F32, BF16, I32, I16 = jnp.float32, jnp.bfloat16, jnp.int32, jnp.int16
VMEM = 48 * 1024 * 1024


def cos_sin(steps, samples):
    eighth = samples // 8
    quadrant = (steps + eighth) >> int(math.log2(samples // 4))
    rest = steps - quadrant * (samples // 4)
    t = rest.astype(F32) * (2.0 * math.pi / samples)
    t2 = t * t
    sine = t + t * t2 * (-1.0 / 6 + t2 * (1.0 / 120 + t2 * (-1.0 / 5040)))
    cosine = 1.0 + t2 * (-0.5 + t2 * (1.0 / 24 + t2 * (-1.0 / 720)))
    odd = (quadrant & 1) == 1
    c = jnp.where(odd, sine, cosine)
    s = jnp.where(odd, cosine, sine)
    c = jnp.where(((quadrant + 1) & 2) == 2, -c, c)
    s = jnp.where((quadrant & 2) == 2, -s, s)
    return c, s


def choose(sizes, pats, pattern, hypo, pick_ref, across, ordered):
    count, entries = pick_ref.shape
    width = min(count, 128)
    for first in range(0, count, width):
        some = slice(first, first + width)
        combo = hypo[some] * pats + pattern[some]
        across[some, :] = jnp.broadcast_to(combo.reshape(1, width), (128, width)).T
    nx, nh, ny, nl, nc = sizes
    for x, h, l, c in np.ndindex(nx, nh, nl, nc):
        source = pl.ds(((x * nh + h) * ny * nl + l) * nc + c, ny, stride=nl * nc)
        place = pl.ds(((c * nl + l) * ny * nh + h) * nx + x, ny, stride=nh * nx)
        ordered[place, :] = across[source, :]
    for first in range(0, entries, 128):
        ids = lax.broadcasted_iota(I32, (count, 128), 1) + first
        pick_ref[:, first : first + 128] = jnp.where(ordered[...] == ids, 1.0, 0.0).astype(BF16)


def merge_kernel(groups, sizes, pats, green_ref, mech_ref, slip_ref, onset_ref, pattern_ref, hypo_ref, msg_ref, pick_ref, green, mech, slip, onset, pattern, hypo, across, ordered, merged, sems):
    _, comps, kinds, subs, freqs = green_ref.shape
    share = freqs // groups
    end = 2 * comps * share
    blocks = [(c, q) for c in range(comps) for q in range(2)]
    copies = [pltpu.make_async_copy(mech_ref, mech, sems.at[0])]
    for i, (c, q) in enumerate(blocks):
        copies.append(pltpu.make_async_copy(green_ref.at[q, c], green.at[i], sems.at[1 + i]))
    copies.append(pltpu.make_async_copy(slip_ref, slip, sems.at[1 + 2 * comps]))
    copies.append(pltpu.make_async_copy(onset_ref, onset, sems.at[2 + 2 * comps]))
    rest = [
        pltpu.make_async_copy(pattern_ref, pattern, sems.at[3 + 2 * comps]),
        pltpu.make_async_copy(hypo_ref, hypo, sems.at[4 + 2 * comps]),
    ]
    for copy in rest + copies[:1] + copies[-2:] + copies[1:-2]:
        copy.start()
    for copy in rest:
        copy.wait()
    choose(sizes, pats, pattern, hypo, pick_ref, across, ordered)
    copies[-2].wait()
    codes = (slip[...].astype(F32) * SLIP_UNIT).astype(I32).astype(I16)
    for g in range(groups):
        msg_ref[g, end + 16 :, :] = codes
    copies[0].wait()
    cols = [jnp.broadcast_to(mech[k : k + 1, :], (subs, subs)).T for k in range(kinds)]
    powers = []

    def merge(i):
        top = jnp.zeros((8, subs), F32)
        for tile in range(freqs // subs):
            piece = slice(tile * subs, (tile + 1) * subs)
            total = cols[0] * green[i, 0, :, piece].astype(F32)
            for k in range(1, kinds):
                total = total + cols[k] * green[i, k, :, piece].astype(F32)
            total = total.T
            merged[i, piece, :] = total
            top = jnp.maximum(top, jnp.max(jnp.abs(total).reshape(subs // 8, 8, subs), axis=0))
        return top

    def encode(i, top):
        most = jnp.maximum(jnp.max(top, axis=0, keepdims=True), LEAST)
        power = jnp.maximum(jnp.ceil(jnp.log2(most * (1.0 / CODE_TOP))), -126.0)
        powers.append(power.astype(I32))
        inverse = jnp.exp2(-power)
        lines = slice(i * share, (i + 1) * share)
        for g in range(groups):
            part = merged[i, pl.ds(g, share, stride=groups), :] * inverse
            msg_ref[g, lines, :] = jnp.round(part).astype(I32).astype(I16)

    for i in range(2 * comps):
        copies[1 + i].wait()
        top = merge(i)
        if i:
            encode(i - 1, before)
        before = top
    encode(2 * comps - 1, before)
    copies[-1].wait()
    for g in range(groups):
        rows = powers + [jnp.full((8 - len(powers), subs), g, I32), onset[...]]
        msg_ref[g, end : end + 16, :] = jnp.concatenate(rows, axis=0).astype(I16)


def table_kernel(groups, samples, msg_ref, pick_ref, out_ref, slips, values, shifted, turns, table, onsets):
    hypos, _, rows = shifted.shape
    subs = values.shape[2]
    pats = slips.shape[0]
    share = rows // 4
    mine = msg_ref[0, rows : rows + 16, :].astype(I32)[4:5]
    freq = mine + groups * lax.broadcasted_iota(I32, (8, subs), 0)

    for src in range(groups):
        lanes = slice(src * subs, (src + 1) * subs)
        slip = msg_ref[src, rows + 16 :, :].astype(I32).astype(F32) * (1.0 / SLIP_UNIT)
        slips[:, lanes] = slip.astype(BF16)
        head = msg_ref[src, rows : rows + 16, :].astype(I32)
        for i in range(4):
            lines = slice(i * share, (i + 1) * share)
            unit = jnp.exp2(head[i : i + 1].astype(F32))
            values[src, lines, :] = msg_ref[src, lines, :].astype(I32).astype(F32) * unit
        onsets[src] = head[8:16]
        near_c, near_s = cos_sin((head[8:16] * (8 * groups)) & (samples - 1), samples)
        turns[src, 0] = near_c
        turns[src, 1] = near_s
        far_c, far_s = near_c * near_c - near_s * near_s, 2.0 * near_c * near_s
        twice_c, twice_s = far_c * far_c - far_s * far_s, 2.0 * far_c * far_s
        turns[src, 2], turns[src, 3] = far_c, far_s
        turns[src, 4], turns[src, 5] = twice_c, twice_s
        turns[src, 6], turns[src, 7] = far_c * twice_c - far_s * twice_s, far_c * twice_s + far_s * twice_c

    spectra = None
    batch = 2
    for h in range(hypos):
        for first in range(0, groups, batch):
            some = slice(first, first + batch)
            onset = jnp.concatenate([jnp.broadcast_to(onsets[src, h : h + 1, :], (8, subs)) for src in range(first, first + batch)], axis=0)
            c0, s0 = cos_sin((onset * jnp.concatenate([freq] * batch, axis=0)) & (samples - 1), samples)
            c0, s0 = c0.reshape(batch, 8, subs), s0.reshape(batch, 8, subs)

            def turned(pair, step):
                jc, js = turns[some, 2 * step, h : h + 1, :], turns[some, 2 * step + 1, h : h + 1, :]
                return pair[0] * jc - pair[1] * js, pair[1] * jc + pair[0] * js

            low = [(c0, s0), turned((c0, s0), 0)]
            real, imag = [[], []], [[], []]
            for a in range(share // 16):
                now = [turned(pair, a) for pair in low] if a else low
                for comp in range(2):
                    re_out, im_out = [], []
                    for half in range(2):
                        c, s = now[half]
                        r0 = comp * 2 * share + a * 16 + half * 8
                        re = values[some, r0 : r0 + 8, :]
                        im = values[some, r0 + share : r0 + share + 8, :]
                        re_out.append(c * re + s * im)
                        im_out.append(c * im - s * re)
                    real[comp].append(jnp.concatenate(re_out, axis=1).astype(BF16))
                    imag[comp].append(jnp.concatenate(im_out, axis=1).astype(BF16))
            for comp in range(2):
                block = jnp.concatenate(real[comp] + imag[comp], axis=1)
                for src in range(first, first + batch):
                    shifted[h, src * subs : (src + 1) * subs, comp * 2 * share : (comp + 1) * 2 * share] = block[src - first].T
        sums = jnp.dot(slips[...], shifted[h], preferred_element_type=F32)
        sums = sums.astype(BF16)
        table[h * pats : (h + 1) * pats, :] = sums
    spectra = jnp.dot(pick_ref[...], table[...], preferred_element_type=F32)
    out_ref[...] = spectra.reshape(out_ref.shape).astype(BF16)


def inverse_tables(groups, freqs, samples):
    share = freqs // groups
    k, b, g, a = np.arange(share), np.arange(128), np.arange(groups), np.arange(samples // 128)
    turn = 2.0 * math.pi / samples
    first = turn * (groups * k[:, None] * b[None, :] % samples)
    c, s = np.cos(first), np.sin(first)
    main = np.concatenate([np.concatenate([c, s], 1), np.concatenate([-s, c], 1)]) / math.sqrt(freqs)
    second = np.tile(turn * (g[:, None] * b[None, :] % samples), (2, 1))
    twist = np.stack([np.cos(second), np.sin(second)])
    third = turn * (128 * g[:, None] * a[None, :] % samples)
    last = np.stack([np.cos(third), -np.sin(third)])[..., None] * np.ones((1, 1, 1, 128))
    main = main.astype(np.float32)
    high = main.astype(ml_dtypes.bfloat16)
    low = (main - high.astype(np.float32)).astype(ml_dtypes.bfloat16)
    main = np.concatenate([high, low, high])
    return [main, twist.astype(np.float32), last.astype(np.float32)]


def inverse_kernel(rings, pair, in_ref, main_ref, twist_ref, last_ref, out_ref):
    count, comps, width = in_ref.shape
    groups = rings * pair
    ring = count // rings
    sums = []
    for x in range(rings):
        part = in_ref[x * ring : (x + 1) * ring].astype(F32).reshape(ring // pair, pair * comps, width)
        sums.append(jnp.sum(part, axis=0))
    sums = jnp.concatenate(sums, axis=0)
    rows = jnp.concatenate([sums[i : i + 1] for comp in range(comps) for i in range(comp, groups * comps, comps)], axis=0)
    row = lax.broadcasted_iota(I32, rows.shape, 0)
    lane = lax.broadcasted_iota(I32, rows.shape, 1)
    zero = (row % groups == 0) & (lane % (width // 2) == 0)
    rows = jnp.where(zero, 0.5 * rows, rows)
    high = rows.astype(BF16)
    low = (rows - high.astype(F32)).astype(BF16)
    v = jnp.dot(jnp.concatenate([high, high, low], axis=1), main_ref[...], preferred_element_type=F32)
    vr, vi = v[:, :128], v[:, 128:]
    c, s = twist_ref[0], twist_ref[1]
    ur, ui = vr * c - vi * s, vr * s + vi * c
    for comp in range(comps):
        total = None
        for g in range(groups):
            r = comp * groups + g
            term = last_ref[0, g] * ur[r : r + 1] + last_ref[1, g] * ui[r : r + 1]
            total = term if total is None else total + term
        for a in range(total.shape[0]):
            out_ref[0, comp : comp + 1, a * 128 : (a + 1) * 128] = total[a : a + 1]


def merge_call(groups, sizes, green, mechanism, slip, onset, pattern, hypo):
    _, comps, kinds, subs, freqs = green.shape
    pats, hypos = slip.shape[0], onset.shape[0]
    lines = 2 * comps * freqs // groups + 16 + pats
    count = pattern.shape[0]
    return pl.pallas_call(
        lambda *refs: merge_kernel(groups, sizes, pats, *refs),
        out_shape=(
            jax.ShapeDtypeStruct((groups, lines, subs), I16),
            jax.ShapeDtypeStruct((count, hypos * pats), BF16),
        ),
        in_specs=[pl.BlockSpec(memory_space=pltpu.HBM)] * 6,
        out_specs=(pl.BlockSpec(memory_space=pltpu.VMEM),) * 2,
        scratch_shapes=[
            pltpu.VMEM((2 * comps, kinds, subs, freqs), BF16),
            pltpu.VMEM((kinds, subs), F32),
            pltpu.VMEM((pats, subs), BF16),
            pltpu.VMEM((hypos, subs), I32),
            pltpu.VMEM((count,), I32),
            pltpu.VMEM((count,), I32),
            pltpu.VMEM((count, 128), I32),
            pltpu.VMEM((count, 128), I32),
            pltpu.VMEM((2 * comps, freqs, subs), F32),
            pltpu.SemaphoreType.DMA((2 * comps + 5,)),
        ],
        compiler_params=pltpu.CompilerParams(vmem_limit_bytes=VMEM),
        name="merge",
    )(*(pltpu.with_memory_space_constraint(v, pltpu.HBM) for v in (green, mechanism, slip, onset, pattern, hypo)))


def table_call(groups, samples, hypos, pats, msg, pick):
    subs = msg.shape[2]
    rows = msg.shape[1] - 16 - pats
    in_vmem = pl.BlockSpec(memory_space=pltpu.VMEM)
    return pl.pallas_call(
        lambda *refs: table_kernel(groups, samples, *refs),
        out_shape=jax.ShapeDtypeStruct((pick.shape[0], rows // 128, 128), BF16),
        in_specs=[in_vmem, in_vmem],
        out_specs=in_vmem,
        scratch_shapes=[
            pltpu.VMEM((pats, groups * subs), BF16),
            pltpu.VMEM((groups, rows, subs), F32),
            pltpu.VMEM((hypos, groups * subs, rows), BF16),
            pltpu.VMEM((groups, 8, hypos, subs), F32),
            pltpu.VMEM((hypos * pats, rows), BF16),
            pltpu.VMEM((groups, hypos, subs), I32),
        ],
        compiler_params=pltpu.CompilerParams(vmem_limit_bytes=VMEM),
        name="table",
    )(msg, pick)


def on_device(green, mechanism, slip, onset, pattern_of_variation, hypo_of_variation):
    _, comps, kinds, subs, freqs = green.shape
    samples = 2 * freqs
    pats, hypos = slip.shape[0], onset.shape[0]
    groups = lax.axis_size(GROUP)
    params = pltpu.CompilerParams(vmem_limit_bytes=VMEM)

    sizes = tuple(lax.axis_size(axis) for axis in AXES)
    msg, pick = merge_call(groups, sizes, green, mechanism, slip, onset, pattern_of_variation, hypo_of_variation)
    msg = lax.all_to_all(msg, GROUP, 0, 0, tiled=True)
    parts = table_call(groups, samples, hypos, pats, msg, pick)
    parts = lax.all_to_all(parts, OWNERS, 0, 0, tiled=True)

    tables = [jnp.asarray(t) for t in inverse_tables(groups, freqs, samples)]
    return pl.pallas_call(
        lambda *refs: inverse_kernel(lax.axis_size("c"), lax.axis_size("x"), *refs),
        out_shape=jax.ShapeDtypeStruct((1, comps, samples), F32),
        compiler_params=params,
        name="inverse",
    )(parts, *tables)


def solution(mesh):
    blk, sub = mesh.devices.shape
    fine = Mesh(mesh.devices.reshape(4, blk // 4, sub // 4, 2, 2), AXES)
    in_specs = (
        P(None, None, None, AXES, None),
        P(None, AXES),
        P(None, AXES),
        P(None, AXES),
        P(),
        P(),
    )
    out_specs = P(AXES, None, None)
    return jax.shard_map(on_device, mesh=fine, in_specs=in_specs, out_specs=out_specs, check_vma=False)
```

```python
import math

import jax
import jax.numpy as jnp
import ml_dtypes
import numpy as np
from jax import lax
from jax.experimental import pallas as pl
from jax.experimental.pallas import tpu as pltpu
from jax.sharding import Mesh
from jax.sharding import PartitionSpec as P

AXES = ("x", "zh", "y", "zl", "c")
GROUP = ("x", "c")
CODE_TOP = 32000.0
SLIP_UNIT = 2048.0
LEAST = 4e-34
F32, BF16, I32, I16 = jnp.float32, jnp.bfloat16, jnp.int32, jnp.int16
VMEM = 48 * 1024 * 1024


def cos_sin(steps, samples):
    eighth = samples // 8
    quadrant = (steps + eighth) >> int(math.log2(samples // 4))
    rest = steps - quadrant * (samples // 4)
    t = rest.astype(F32) * (2.0 * math.pi / samples)
    t2 = t * t
    sine = t + t * t2 * (-1.0 / 6 + t2 * (1.0 / 120 + t2 * (-1.0 / 5040)))
    cosine = 1.0 + t2 * (-0.5 + t2 * (1.0 / 24 + t2 * (-1.0 / 720)))
    odd = (quadrant & 1) == 1
    c = jnp.where(odd, sine, cosine)
    s = jnp.where(odd, cosine, sine)
    c = jnp.where(((quadrant + 1) & 2) == 2, -c, c)
    s = jnp.where((quadrant & 2) == 2, -s, s)
    return c, s


def choose(pats, pattern, hypo, pick_ref, across):
    count, entries = pick_ref.shape
    width = min(count, 128)
    for first in range(0, count, width):
        some = slice(first, first + width)
        combo = hypo[some] * pats + pattern[some]
        across[some, :] = jnp.broadcast_to(combo.reshape(1, width), (128, width)).T
    for first in range(0, entries, 128):
        ids = lax.broadcasted_iota(I32, (count, 128), 1) + first
        pick_ref[:, first : first + 128] = jnp.where(across[...] == ids, 1.0, 0.0).astype(BF16)


def merge_kernel(groups, pats, green_ref, mech_ref, slip_ref, onset_ref, pattern_ref, hypo_ref, msg_ref, pick_ref, green, mech, slip, onset, pattern, hypo, across, merged, sems):
    _, comps, kinds, subs, freqs = green_ref.shape
    share = freqs // groups
    end = 2 * comps * share
    blocks = [(c, q) for c in range(comps) for q in range(2)]
    copies = [pltpu.make_async_copy(mech_ref, mech, sems.at[0])]
    for i, (c, q) in enumerate(blocks):
        copies.append(pltpu.make_async_copy(green_ref.at[q, c], green.at[i], sems.at[1 + i]))
    copies.append(pltpu.make_async_copy(slip_ref, slip, sems.at[1 + 2 * comps]))
    copies.append(pltpu.make_async_copy(onset_ref, onset, sems.at[2 + 2 * comps]))
    rest = [
        pltpu.make_async_copy(pattern_ref, pattern, sems.at[3 + 2 * comps]),
        pltpu.make_async_copy(hypo_ref, hypo, sems.at[4 + 2 * comps]),
    ]
    for copy in rest + copies[:1] + copies[-2:] + copies[1:-2]:
        copy.start()
    for copy in rest:
        copy.wait()
    choose(pats, pattern, hypo, pick_ref, across)
    copies[-2].wait()
    codes = (slip[...].astype(F32) * SLIP_UNIT).astype(I32).astype(I16)
    for g in range(groups):
        msg_ref[g, end + 16 :, :] = codes
    copies[0].wait()
    cols = [jnp.broadcast_to(mech[k : k + 1, :], (subs, subs)).T for k in range(kinds)]
    powers = []

    def merge(i):
        top = jnp.zeros((8, subs), F32)
        for first in range(0, freqs, 2 * subs):
            piece = slice(first, first + 2 * subs)
            wide = [jnp.concatenate([col] * 2, axis=1) for col in cols]
            total = wide[0] * green[i, 0, :, piece].astype(F32)
            for k in range(1, kinds):
                total = total + wide[k] * green[i, k, :, piece].astype(F32)
            total = total.T
            merged[i, piece, :] = total
            top = jnp.maximum(top, jnp.max(jnp.abs(total).reshape(-1, 8, subs), axis=0))
        return top

    def encode(i, top):
        most = jnp.maximum(jnp.max(top, axis=0, keepdims=True), LEAST)
        power = jnp.maximum(jnp.ceil(jnp.log2(most * (1.0 / CODE_TOP))), -126.0)
        powers.append(power.astype(I32))
        inverse = jnp.exp2(-power)
        lines = slice(i * share, (i + 1) * share)
        for g in range(groups):
            part = merged[i, pl.ds(g, share, stride=groups), :] * inverse
            msg_ref[g, lines, :] = jnp.round(part).astype(I32).astype(I16)

    for i in range(2 * comps):
        copies[1 + i].wait()
        top = merge(i)
        if i:
            encode(i - 1, before)
        before = top
    encode(2 * comps - 1, before)
    copies[-1].wait()
    for g in range(groups):
        rows = powers + [jnp.full((8 - len(powers), subs), g, I32), onset[...]]
        msg_ref[g, end : end + 16, :] = jnp.concatenate(rows, axis=0).astype(I16)


def table_kernel(groups, samples, msg_ref, pick_ref, out_ref, slips, values, shifted, turns, table, onsets):
    hypos, _, rows = shifted.shape
    subs = values.shape[2]
    pats = slips.shape[0]
    share = rows // 4
    mine = msg_ref[0, rows : rows + 16, :].astype(I32)[4:5]
    freq = mine + groups * lax.broadcasted_iota(I32, (8, subs), 0)

    for src in range(groups):
        lanes = slice(src * subs, (src + 1) * subs)
        slip = msg_ref[src, rows + 16 :, :].astype(I32).astype(F32) * (1.0 / SLIP_UNIT)
        slips[:, lanes] = slip.astype(BF16)
        head = msg_ref[src, rows : rows + 16, :].astype(I32)
        for i in range(4):
            lines = slice(i * share, (i + 1) * share)
            unit = jnp.exp2(head[i : i + 1].astype(F32))
            values[src, lines, :] = msg_ref[src, lines, :].astype(I32).astype(F32) * unit
        onsets[src] = head[8:16]
        near_c, near_s = cos_sin((head[8:16] * (8 * groups)) & (samples - 1), samples)
        turns[src, 0] = near_c
        turns[src, 1] = near_s
        far_c, far_s = near_c * near_c - near_s * near_s, 2.0 * near_c * near_s
        twice_c, twice_s = far_c * far_c - far_s * far_s, 2.0 * far_c * far_s
        turns[src, 2], turns[src, 3] = far_c, far_s
        turns[src, 4], turns[src, 5] = twice_c, twice_s
        turns[src, 6], turns[src, 7] = far_c * twice_c - far_s * twice_s, far_c * twice_s + far_s * twice_c

    spectra = None
    batch = 2
    for h in range(hypos):
        for first in range(0, groups, batch):
            some = slice(first, first + batch)
            onset = jnp.concatenate([jnp.broadcast_to(onsets[src, h : h + 1, :], (8, subs)) for src in range(first, first + batch)], axis=0)
            c0, s0 = cos_sin((onset * jnp.concatenate([freq] * batch, axis=0)) & (samples - 1), samples)
            c0, s0 = c0.reshape(batch, 8, subs), s0.reshape(batch, 8, subs)

            def turned(pair, step):
                jc, js = turns[some, 2 * step, h : h + 1, :], turns[some, 2 * step + 1, h : h + 1, :]
                return pair[0] * jc - pair[1] * js, pair[1] * jc + pair[0] * js

            low = [(c0, s0), turned((c0, s0), 0)]
            real, imag = [[], []], [[], []]
            for a in range(share // 16):
                now = [turned(pair, a) for pair in low] if a else low
                for comp in range(2):
                    re_out, im_out = [], []
                    for half in range(2):
                        c, s = now[half]
                        r0 = comp * 2 * share + a * 16 + half * 8
                        re = values[some, r0 : r0 + 8, :]
                        im = values[some, r0 + share : r0 + share + 8, :]
                        re_out.append(c * re + s * im)
                        im_out.append(c * im - s * re)
                    real[comp].append(jnp.concatenate(re_out, axis=1).astype(BF16))
                    imag[comp].append(jnp.concatenate(im_out, axis=1).astype(BF16))
            for src in range(first, first + batch):
                block = jnp.concatenate([part[src - first] for comp in range(2) for part in real[comp] + imag[comp]], axis=0)
                shifted[h, src * subs : (src + 1) * subs, :] = block.T
        sums = jnp.dot(slips[...], shifted[h], preferred_element_type=F32)
        sums = sums.astype(BF16)
        table[h * pats : (h + 1) * pats, :] = sums
    spectra = jnp.dot(pick_ref[...], table[...], preferred_element_type=F32)
    out_ref[...] = spectra.reshape(out_ref.shape).astype(BF16)


def inverse_tables(groups, freqs, samples):
    share = freqs // groups
    k, b, g, a = np.arange(share), np.arange(128), np.arange(groups), np.arange(samples // 128)
    turn = 2.0 * math.pi / samples
    first = turn * (groups * k[:, None] * b[None, :] % samples)
    c, s = np.cos(first), np.sin(first)
    main = np.concatenate([np.concatenate([c, s], 1), np.concatenate([-s, c], 1)]) / math.sqrt(freqs)
    second = np.tile(turn * (g[:, None] * b[None, :] % samples), (2, 1))
    twist = np.stack([np.cos(second), np.sin(second)])
    third = turn * (128 * g[:, None] * a[None, :] % samples)
    last = np.stack([np.cos(third), -np.sin(third)])[..., None] * np.ones((1, 1, 1, 128))
    main = main.astype(np.float32)
    high = main.astype(ml_dtypes.bfloat16)
    low = (main - high.astype(np.float32)).astype(ml_dtypes.bfloat16)
    main = np.concatenate([high, low, high])
    return [main, twist.astype(np.float32), last.astype(np.float32)]


def inverse_kernel(rings, pair, in_ref, main_ref, twist_ref, last_ref, out_ref):
    count, comps, width = in_ref.shape
    groups = rings * pair
    ring = count // rings
    sums = []
    for x in range(rings):
        part = in_ref[x * ring : (x + 1) * ring].astype(F32).reshape(ring // pair, pair * comps, width)
        sums.append(jnp.sum(part, axis=0))
    sums = jnp.concatenate(sums, axis=0)
    rows = jnp.concatenate([sums[i : i + 1] for comp in range(comps) for i in range(comp, groups * comps, comps)], axis=0)
    row = lax.broadcasted_iota(I32, rows.shape, 0)
    lane = lax.broadcasted_iota(I32, rows.shape, 1)
    zero = (row % groups == 0) & (lane % (width // 2) == 0)
    rows = jnp.where(zero, 0.5 * rows, rows)
    high = rows.astype(BF16)
    low = (rows - high.astype(F32)).astype(BF16)
    v = jnp.dot(jnp.concatenate([high, high, low], axis=1), main_ref[...], preferred_element_type=F32)
    vr, vi = v[:, :128], v[:, 128:]
    c, s = twist_ref[0], twist_ref[1]
    ur, ui = vr * c - vi * s, vr * s + vi * c
    for comp in range(comps):
        total = None
        for g in range(groups):
            r = comp * groups + g
            term = last_ref[0, g] * ur[r : r + 1] + last_ref[1, g] * ui[r : r + 1]
            total = term if total is None else total + term
        for a in range(total.shape[0]):
            out_ref[0, comp : comp + 1, a * 128 : (a + 1) * 128] = total[a : a + 1]


def merge_call(groups, green, mechanism, slip, onset, pattern, hypo):
    _, comps, kinds, subs, freqs = green.shape
    pats, hypos = slip.shape[0], onset.shape[0]
    lines = 2 * comps * freqs // groups + 16 + pats
    count = pattern.shape[0]
    return pl.pallas_call(
        lambda *refs: merge_kernel(groups, pats, *refs),
        out_shape=(
            jax.ShapeDtypeStruct((groups, lines, subs), I16),
            jax.ShapeDtypeStruct((count, hypos * pats), BF16),
        ),
        in_specs=[pl.BlockSpec(memory_space=pltpu.HBM)] * 6,
        out_specs=(pl.BlockSpec(memory_space=pltpu.VMEM),) * 2,
        scratch_shapes=[
            pltpu.VMEM((2 * comps, kinds, subs, freqs), BF16),
            pltpu.VMEM((kinds, subs), F32),
            pltpu.VMEM((pats, subs), BF16),
            pltpu.VMEM((hypos, subs), I32),
            pltpu.VMEM((count,), I32),
            pltpu.VMEM((count,), I32),
            pltpu.VMEM((count, 128), I32),
            pltpu.VMEM((2 * comps, freqs, subs), F32),
            pltpu.SemaphoreType.DMA((2 * comps + 5,)),
        ],
        compiler_params=pltpu.CompilerParams(vmem_limit_bytes=VMEM),
        name="merge",
    )(*(pltpu.with_memory_space_constraint(v, pltpu.HBM) for v in (green, mechanism, slip, onset, pattern, hypo)))


def table_call(groups, samples, hypos, pats, msg, pick):
    subs = msg.shape[2]
    rows = msg.shape[1] - 16 - pats
    in_vmem = pl.BlockSpec(memory_space=pltpu.VMEM)
    return pl.pallas_call(
        lambda *refs: table_kernel(groups, samples, *refs),
        out_shape=jax.ShapeDtypeStruct((pick.shape[0], rows // 128, 128), BF16),
        in_specs=[in_vmem, in_vmem],
        out_specs=in_vmem,
        scratch_shapes=[
            pltpu.VMEM((pats, groups * subs), BF16),
            pltpu.VMEM((groups, rows, subs), F32),
            pltpu.VMEM((hypos, groups * subs, rows), BF16),
            pltpu.VMEM((groups, 8, hypos, subs), F32),
            pltpu.VMEM((hypos * pats, rows), BF16),
            pltpu.VMEM((groups, hypos, subs), I32),
        ],
        compiler_params=pltpu.CompilerParams(vmem_limit_bytes=VMEM),
        name="table",
    )(msg, pick)


def on_device(green, mechanism, slip, onset, pattern_of_variation, hypo_of_variation):
    _, comps, kinds, subs, freqs = green.shape
    samples = 2 * freqs
    pats, hypos = slip.shape[0], onset.shape[0]
    groups = lax.axis_size(GROUP)
    params = pltpu.CompilerParams(vmem_limit_bytes=VMEM)

    msg, pick = merge_call(groups, green, mechanism, slip, onset, pattern_of_variation, hypo_of_variation)
    msg = lax.all_to_all(msg, GROUP, 0, 0, tiled=True)
    parts = table_call(groups, samples, hypos, pats, msg, pick)
    parts = lax.all_to_all(parts, AXES, 0, 0, tiled=True)

    tables = [jnp.asarray(t) for t in inverse_tables(groups, freqs, samples)]
    return pl.pallas_call(
        lambda *refs: inverse_kernel(lax.axis_size("x"), lax.axis_size("c"), *refs),
        out_shape=jax.ShapeDtypeStruct((1, comps, samples), F32),
        compiler_params=params,
        name="inverse",
    )(parts, *tables)


def solution(mesh):
    blk, sub = mesh.devices.shape
    fine = Mesh(mesh.devices.reshape(4, blk // 4, sub // 4, 2, 2), AXES)
    in_specs = (
        P(None, None, None, AXES, None),
        P(None, AXES),
        P(None, AXES),
        P(None, AXES),
        P(),
        P(),
    )
    out_specs = P(AXES, None, None)
    return jax.shard_map(on_device, mesh=fine, in_specs=in_specs, out_specs=out_specs, check_vma=False)
```
